1024 devices in a mesh: dp: 256 (over y, x, z_lo, core), fsdp: 4 (over z_hi).
Axes of the slice: x: 4, y: 4, z: 32 (z_hi: 4, z_lo: 8; z = z_hi * 8 + z_lo), core: 2. Of those that a mesh axis runs over, the one named last changes fastest.
Arguments:
- img_raw: bfloat16 [131072, 1536], P(('dp', 'fsdp')), may hold values from -0.15625 to 0.15625
- txt_raw: bfloat16 [131072, 1536], P(('dp', 'fsdp')), may hold values from -0.15625 to 0.15625
- logit_scale: float32 [], replicated, may hold values from 2 to 8
- logit_bias: float32 [], replicated, may hold values from -4 to -1
Outputs:
- img_grad: bfloat16 [131072, 1536], P(('dp', 'fsdp'))
- txt_grad: bfloat16 [131072, 1536], P(('dp', 'fsdp'))
The draws below stay inside these ranges and needn't reach their ends.
All inputs are finite; a program needn't handle non-finite values.
Results may differ from the reference program's by a relative error of at most 0.015.
Values may be sent and summed in bfloat16 or wider, within the bound.
No kernel may reach another device: no remote copies, remote signals or barrier semaphores. Data moves between devices by JAX's collectives and lax.ppermute only.
A program may use at most 32 MiB of HBM per device.

```python
import jax
import jax.numpy as jnp
from jax import lax

E = 1536
B_DP = 512
HALF = 1
PAIRS = 131072
N_DP = 256


def level_of(rng, dims, split, smallest, high):
    factor_of = 1.0
    for position, blocks in split:
        heights = jax.random.uniform(jax.random.fold_in(jax.random.fold_in(rng, 6), position), (blocks,), jnp.float32, smallest / len(split), high / len(split))
        factor_of = factor_of * jnp.repeat(jnp.exp(heights), dims[position] // blocks).reshape((-1,) + (1,) * (len(dims) - 1 - position))
    return factor_of


def noise(key, dims, scale, bound, shards=(), kind=jnp.bfloat16):
    values = jax.random.normal(key, dims, jnp.float32) * scale
    if len(shards) > 0:
        values = level_of(key, dims, shards, -0.22, 0.18) * values
    return jnp.clip(values, min=-bound, max=bound).astype(kind)


def setup_inputs(seed: int = 0) -> dict:
    streams_of = jax.random.split(jax.random.key(seed), 5)
    img_raw = noise(streams_of[0], (PAIRS, E), E ** -0.5, 0.15625, ((0, 1024),))
    txt_raw = noise(streams_of[1], (PAIRS, E), E ** -0.5, 0.15625, ((0, 1024),))
    logit_scale = jnp.clip(jax.random.uniform(streams_of[2], (), jnp.float32, 2.0, 8.0), 2.0, 8.0)
    logit_bias = jnp.clip(jax.random.uniform(streams_of[3], (), jnp.float32, -4.0, -1.0), -4.0, -1.0)
    return dict(img_raw=img_raw, txt_raw=txt_raw, logit_scale=logit_scale, logit_bias=logit_bias)


def normalize(raw):
    values = raw.astype(jnp.float32)
    inverse = lax.rsqrt(lax.optimization_barrier(jnp.sum(values * values, axis=-1, keepdims=True)) + 1e-06)
    return (values * inverse, inverse)

def unnormalize(normed, inverse, direction):
    inner = lax.optimization_barrier(jnp.sum(normed * direction, axis=-1, keepdims=True))
    return (direction - normed * inner) * inverse

def reference(img_raw, txt_raw, logit_scale, logit_bias):
    img_norm, img_inv = normalize(img_raw.reshape(N_DP, B_DP, E))
    txt_norm, txt_inv = normalize(txt_raw.reshape(N_DP, B_DP, E))
    img_low = img_norm.astype(jnp.bfloat16).astype(jnp.float32)
    txt_low = txt_norm.astype(jnp.bfloat16).astype(jnp.float32)
    identity = jnp.eye(B_DP, dtype=jnp.float32)
    img_dir = jnp.zeros((N_DP, B_DP, E), jnp.float32)
    txt_dir = jnp.zeros((N_DP, B_DP, E), jnp.float32)
    for offset in range(-HALF, HALF + 1):
        met = jnp.roll(txt_low, offset, axis=0)
        logits = logit_scale * jnp.einsum('abe,ace->abc', img_low, met) + logit_bias
        if offset == 0:
            labels = 2.0 * identity - 1.0
        else:
            labels = -jnp.ones((B_DP, B_DP), jnp.float32)
        coef = (-labels * jax.nn.sigmoid(-labels * logits) * logit_scale).astype(jnp.bfloat16).astype(jnp.float32)
        img_dir = img_dir + jnp.einsum('abc,ace->abe', coef, met)
        txt_term = jnp.einsum('abc,abe->ace', coef, img_low)
        txt_dir = txt_dir + jnp.roll(txt_term, -offset, axis=0)
    img_grad = unnormalize(img_norm, img_inv, img_dir).astype(jnp.bfloat16)
    txt_grad = unnormalize(txt_norm, txt_inv, txt_dir).astype(jnp.bfloat16)
    return (img_grad.reshape(PAIRS, E), txt_grad.reshape(PAIRS, E))
```

```python
import jax
import jax.numpy as jnp
from jax import lax
from jax.sharding import PartitionSpec as P

AXES = ("dp", "fsdp")
SPAN = 16


def device_of(block, role, blocks, ways):
    block = block % blocks
    return block * ways + (role + block // SPAN) % ways


def routes(blocks, ways):
    img, txt, ahead, back = [], [], [], []
    for block in range(blocks):
        for role in range(ways):
            here = device_of(block, role, blocks, ways)
            img.append((here, device_of(block, role ^ 1, blocks, ways)))
            txt.append((here, device_of(block, ways - 1 - role, blocks, ways)))
            ahead.append((here, device_of(block + 1, role, blocks, ways)))
            back.append((here, device_of(block - 1, role, blocks, ways)))
    return img, txt, ahead, back


def normalize(raw):
    values = raw.astype(jnp.float32)
    inverse = lax.rsqrt(jnp.sum(values * values, axis=-1, keepdims=True) + 1e-06)
    return (values * inverse, inverse)


def low(raw):
    return normalize(raw)[0].astype(jnp.bfloat16)


def grad_of(raw, direction):
    norm, inverse = normalize(raw)
    inner = jnp.sum(norm * direction, axis=-1, keepdims=True)
    return ((direction - norm * inner) * inverse).astype(jnp.bfloat16)


def pair_coef(img, txt, logit_scale, logit_bias, labels):
    scores = lax.dot_general(
        img, txt, (((1,), (1,)), ((), ())), preferred_element_type=jnp.float32
    )
    logits = logit_scale * scores + logit_bias
    return (-labels * jax.nn.sigmoid(-labels * logits) * logit_scale).astype(jnp.bfloat16)


def img_part(coef, txt):
    return jnp.dot(coef, txt, preferred_element_type=jnp.float32)


def txt_part(coef, img):
    return lax.dot_general(
        coef, img, (((0,), (0,)), ((), ())), preferred_element_type=jnp.float32
    )


def local(img_raw, txt_raw, logit_scale, logit_bias, moves):
    to_img, to_txt, ahead, back = moves
    rows = img_raw.shape[0]
    txt_far = lax.ppermute(txt_raw, AXES, to_txt)
    img_far = lax.ppermute(img_raw, AXES, to_img)
    prev_own = lax.ppermute(txt_raw, AXES, ahead)
    next_own = lax.ppermute(txt_raw, AXES, back)
    prev_far = lax.ppermute(txt_far, AXES, ahead)
    next_far = lax.ppermute(txt_far, AXES, back)

    img = jnp.concatenate([low(img_raw), low(img_far)])
    txt = jnp.concatenate([low(txt_raw), low(txt_far)])
    prev = jnp.concatenate([low(prev_own), low(prev_far)])
    following = jnp.concatenate([low(next_own), low(next_far)])

    shape = (2 * rows, 2 * rows)
    first = lax.broadcasted_iota(jnp.int32, shape, 0)
    positive = (first == lax.broadcasted_iota(jnp.int32, shape, 1)) & (first < rows)
    labels = jnp.where(positive, 1.0, -1.0).astype(jnp.float32)
    negative = jnp.float32(-1.0)
    coef_prev = pair_coef(img, prev, logit_scale, logit_bias, negative)
    coef_next = pair_coef(img, following, logit_scale, logit_bias, negative)
    coef_own = pair_coef(img, txt, logit_scale, logit_bias, labels)

    to_prev = txt_part(coef_prev, img).astype(jnp.bfloat16)
    to_next = txt_part(coef_next, img).astype(jnp.bfloat16)
    from_next_far = lax.ppermute(to_prev[rows:], AXES, back)
    from_prev_far = lax.ppermute(to_next[rows:], AXES, ahead)
    img_dir = img_part(coef_prev, prev) + img_part(coef_own, txt) + img_part(coef_next, following)
    img_there = lax.ppermute(img_dir[rows:].astype(jnp.bfloat16), AXES, to_img)
    from_next_own = lax.ppermute(to_prev[:rows], AXES, back)
    from_prev_own = lax.ppermute(to_next[:rows], AXES, ahead)
    own = txt_part(coef_own, img)
    far_sum = own[rows:] + from_next_far.astype(jnp.float32) + from_prev_far.astype(jnp.float32)
    txt_there = lax.ppermute(far_sum.astype(jnp.bfloat16), AXES, to_txt)
    own_sum = own[:rows] + from_next_own.astype(jnp.float32) + from_prev_own.astype(jnp.float32)

    img_grad = grad_of(img_raw, img_dir[:rows] + img_there.astype(jnp.float32))
    txt_grad = grad_of(txt_raw, own_sum + txt_there.astype(jnp.float32))
    return (img_grad, txt_grad)


def solution(mesh):
    moves = routes(mesh.shape["dp"], mesh.shape["fsdp"])
    in_specs = (P(AXES, None), P(AXES, None), P(), P())
    out_specs = (P(AXES, None), P(AXES, None))

    def step(*args):
        return local(*args, moves)

    return jax.shard_map(step, mesh=mesh, in_specs=in_specs, out_specs=out_specs, check_vma=False)
```

```python
import jax
import jax.numpy as jnp
from jax import lax
from jax.sharding import PartitionSpec as P

AXES = ("dp", "fsdp")
SPAN = 16


def device_of(block, role, blocks, ways):
    block = block % blocks
    return block * ways + (role + block // SPAN) % ways


def routes(blocks, ways):
    img, txt, ahead, back = [], [], [], []
    for block in range(blocks):
        for role in range(ways):
            here = device_of(block, role, blocks, ways)
            img.append((here, device_of(block, role ^ 1, blocks, ways)))
            txt.append((here, device_of(block, ways - 1 - role, blocks, ways)))
            ahead.append((here, device_of(block + 1, role, blocks, ways)))
            back.append((here, device_of(block - 1, role, blocks, ways)))
    return img, txt, ahead, back


def normalize(raw):
    values = raw.astype(jnp.float32)
    inverse = lax.rsqrt(jnp.sum(values * values, axis=-1, keepdims=True) + 1e-06)
    return (values * inverse, inverse)


def low(raw):
    return normalize(raw)[0].astype(jnp.bfloat16)


def grad_of(raw, direction):
    norm, inverse = normalize(raw)
    inner = jnp.sum(norm * direction, axis=-1, keepdims=True)
    return ((direction - norm * inner) * inverse).astype(jnp.bfloat16)


def pair_coef(img, txt, logit_scale, logit_bias, labels):
    scores = lax.dot_general(
        img, txt, (((1,), (1,)), ((), ())), preferred_element_type=jnp.float32
    )
    logits = logit_scale * scores + logit_bias
    return (-labels * jax.nn.sigmoid(-labels * logits) * logit_scale).astype(jnp.bfloat16)


def img_part(coef, txt):
    return jnp.dot(coef, txt, preferred_element_type=jnp.float32)


def txt_part(coef, img):
    return lax.dot_general(
        coef, img, (((0,), (0,)), ((), ())), preferred_element_type=jnp.float32
    )


def local(img_raw, txt_raw, logit_scale, logit_bias, moves):
    to_img, to_txt, ahead, back = moves
    rows = img_raw.shape[0]
    txt_far = lax.ppermute(txt_raw, AXES, to_txt)
    img_far = lax.ppermute(img_raw, AXES, to_img)

    def half(own, far, route):
        return jnp.concatenate(
            [low(lax.ppermute(own, AXES, route)), low(lax.ppermute(far, AXES, route))]
        )

    img = jnp.concatenate([low(img_raw), low(img_far)])
    txt = jnp.concatenate([low(txt_raw), low(txt_far)])
    img_prev, img_next = half(img_raw, img_far, ahead), half(img_raw, img_far, back)
    txt_prev, txt_next = half(txt_raw, txt_far, ahead), half(txt_raw, txt_far, back)

    shape = (2 * rows, 2 * rows)
    first = lax.broadcasted_iota(jnp.int32, shape, 0)
    positive = (first == lax.broadcasted_iota(jnp.int32, shape, 1)) & (first < rows)
    labels = jnp.where(positive, 1.0, -1.0).astype(jnp.float32)
    negative = jnp.float32(-1.0)

    def coef(images, texts, signs):
        return pair_coef(images, texts, logit_scale, logit_bias, signs)

    own = coef(img, txt, labels)
    img_dir = (
        img_part(own, txt)
        + img_part(coef(img, txt_prev, negative), txt_prev)
        + img_part(coef(img, txt_next, negative), txt_next)
    )
    txt_dir = (
        txt_part(own, img)
        + txt_part(coef(img_prev, txt, negative), img_prev)
        + txt_part(coef(img_next, txt, negative), img_next)
    )
    img_there = lax.ppermute(img_dir[rows:].astype(jnp.bfloat16), AXES, to_img)
    txt_there = lax.ppermute(txt_dir[rows:].astype(jnp.bfloat16), AXES, to_txt)
    img_grad = grad_of(img_raw, img_dir[:rows] + img_there.astype(jnp.float32))
    txt_grad = grad_of(txt_raw, txt_dir[:rows] + txt_there.astype(jnp.float32))
    return (img_grad, txt_grad)


def solution(mesh):
    moves = routes(mesh.shape["dp"], mesh.shape["fsdp"])
    in_specs = (P(AXES, None), P(AXES, None), P(), P())
    out_specs = (P(AXES, None), P(AXES, None))

    def step(*args):
        return local(*args, moves)

    return jax.shard_map(step, mesh=mesh, in_specs=in_specs, out_specs=out_specs, check_vma=False)
```

```python
import jax
import jax.numpy as jnp
from jax import lax
from jax.experimental import pallas as pl
from jax.experimental.pallas import tpu as pltpu
from jax.sharding import PartitionSpec as P

AXES = ("dp", "fsdp")
SPAN = 16
STRIP = 32
VMEM_LIMIT = 32 * 1024 * 1024


def device_of(block, role, blocks, ways):
    block = block % blocks
    return block * ways + (role + block // SPAN) % ways


def routes(blocks, ways):
    img, txt, mate, cross = [], [], [], []
    for block in range(blocks):
        for role in range(ways):
            here = device_of(block, role, blocks, ways)
            across = block + 1 if block % 2 else block - 1
            img.append((here, device_of(block, role ^ 1, blocks, ways)))
            txt.append((here, device_of(block, ways - 1 - role, blocks, ways)))
            mate.append((here, device_of(block ^ 1, role, blocks, ways)))
            cross.append((here, device_of(across, role, blocks, ways)))
    return img, txt, mate, cross


def inverse_of(values):
    return lax.rsqrt(jnp.sum(values * values, axis=-1, keepdims=True) + 1e-06)


def low_kernel(img_ref, txt_ref, low_ref):
    rows = img_ref.shape[0]
    for part, ref in enumerate((img_ref, txt_ref)):
        for start in range(0, rows, STRIP):
            values = ref[start : start + STRIP, :].astype(jnp.float32)
            strip = (values * inverse_of(values)).astype(jnp.bfloat16)
            low_ref[part * rows + start : part * rows + start + STRIP, :] = strip


def scores_of(left, right):
    return lax.dot_general(left, right, (((1,), (1,)), ((), ())), preferred_element_type=jnp.float32)


def negative_coef(left, right, scale, bias):
    return (jax.nn.sigmoid(scale * scores_of(left, right) + bias) * scale).astype(jnp.bfloat16)


def columns_of(width, step=256):
    return [slice(start, start + step) for start in range(0, width, step)]


def stack(first, second, part, rows, out_ref):
    out_ref[:rows, :] = first[part * rows : (part + 1) * rows, :]
    out_ref[rows:, :] = second[part * rows : (part + 1) * rows, :]


def near_kernel(scale_ref, bias_ref, own, far, mate, cross, img_acc, txt_acc, img, txt, img_n, txt_n):
    rows = own.shape[0] // 2
    scale, bias = scale_ref[0], bias_ref[0]
    stack(own, far, 0, rows, img)
    stack(own, far, 1, rows, txt)
    stack(mate, cross, 0, rows, img_n)
    stack(mate, cross, 1, rows, txt_n)

    shape = (2 * rows, 2 * rows)
    first = lax.broadcasted_iota(jnp.int32, shape, 0)
    positive = (first == lax.broadcasted_iota(jnp.int32, shape, 1)) & (first < rows)
    logits = scale * scores_of(img[...], txt[...]) + bias
    size = jax.nn.sigmoid(jnp.where(positive, -logits, logits)) * scale
    signed = jnp.where(positive, -size, size)
    coef_own = signed.astype(jnp.bfloat16)
    coef_own_t = signed.T.astype(jnp.bfloat16)
    coef_img = negative_coef(img[...], txt_n[...], scale, bias)
    coef_txt = negative_coef(txt[...], img_n[...], scale, bias)

    def dot(coef, ref, cols):
        return jnp.dot(coef, ref[:, cols], preferred_element_type=jnp.float32)

    for cols in columns_of(own.shape[1]):
        img_acc[:, cols] = dot(coef_own, txt, cols) + dot(coef_img, txt_n, cols)
        txt_acc[:, cols] = dot(coef_own_t, img, cols) + dot(coef_txt, img_n, cols)


def far_kernel(
    scale_ref, bias_ref, own, far, mate, cross, img_acc, txt_acc,
    img_own, img_far, txt_own, txt_far, img, txt, img_n, txt_n,
):
    rows = own.shape[0] // 2
    scale, bias = scale_ref[0], bias_ref[0]
    stack(own, far, 0, rows, img)
    stack(own, far, 1, rows, txt)
    stack(mate, cross, 0, rows, img_n)
    stack(mate, cross, 1, rows, txt_n)
    coef_img = negative_coef(img[...], txt_n[...], scale, bias)
    coef_txt = negative_coef(txt[...], img_n[...], scale, bias)
    for cols in columns_of(own.shape[1]):
        total = img_acc[:, cols] + jnp.dot(
            coef_img, txt_n[:, cols], preferred_element_type=jnp.float32
        )
        img_own[:, cols] = total[:rows]
        img_far[:, cols] = total[rows:].astype(jnp.bfloat16)
        total = txt_acc[:, cols] + jnp.dot(
            coef_txt, img_n[:, cols], preferred_element_type=jnp.float32
        )
        txt_own[:, cols] = total[:rows]
        txt_far[:, cols] = total[rows:].astype(jnp.bfloat16)


def grad_kernel(raw_ref, own_ref, there_ref, out_ref):
    for start in range(0, raw_ref.shape[0], STRIP):
        here = slice(start, start + STRIP)
        values = raw_ref[here, :].astype(jnp.float32)
        inverse = inverse_of(values)
        norm = values * inverse
        direction = own_ref[here, :] + there_ref[here, :].astype(jnp.float32)
        inner = jnp.sum(norm * direction, axis=-1, keepdims=True)
        out_ref[here, :] = ((direction - norm * inner) * inverse).astype(jnp.bfloat16)


def call(kernel, outs, scalars, arrays, scratch=(), flops=0):
    moved = sum(a.size * a.dtype.itemsize for a in arrays)
    return pl.pallas_call(
        kernel,
        out_shape=outs,
        in_specs=[pl.BlockSpec(memory_space=pltpu.SMEM)] * len(scalars)
        + [pl.BlockSpec(memory_space=pltpu.VMEM)] * len(arrays),
        out_specs=jax.tree.map(lambda _: pl.BlockSpec(memory_space=pltpu.VMEM), outs),
        scratch_shapes=list(scratch),
        compiler_params=pltpu.CompilerParams(vmem_limit_bytes=VMEM_LIMIT),
        cost_estimate=pl.CostEstimate(flops=flops, bytes_accessed=moved, transcendentals=0),
    )(*scalars, *arrays)


def local(img_raw, txt_raw, logit_scale, logit_bias, moves):
    to_img, to_txt, to_mate, to_cross = moves
    rows, width = img_raw.shape
    scalars = (logit_scale.reshape(1), logit_bias.reshape(1))
    low_shape = jax.ShapeDtypeStruct((2 * rows, width), jnp.bfloat16)
    acc_shape = jax.ShapeDtypeStruct((2 * rows, width), jnp.float32)
    own_shape = jax.ShapeDtypeStruct((rows, width), jnp.float32)
    sent_shape = jax.ShapeDtypeStruct((rows, width), jnp.bfloat16)
    halves = [pltpu.VMEM((2 * rows, width), jnp.bfloat16)] * 4
    unit = 2 * (2 * rows) * (2 * rows) * width

    img_there = lax.ppermute(img_raw, AXES, to_img)
    txt_there = lax.ppermute(txt_raw, AXES, to_txt)
    own = call(low_kernel, low_shape, (), (img_raw, txt_raw))
    cross_own = lax.ppermute(own, AXES, to_cross)
    mate_own = lax.ppermute(own, AXES, to_mate)
    far = call(low_kernel, low_shape, (), (img_there, txt_there))
    cross_far = lax.ppermute(far, AXES, to_cross)
    mate_far = lax.ppermute(far, AXES, to_mate)
    img_acc, txt_acc = call(
        near_kernel, (acc_shape, acc_shape), scalars, (own, far, mate_own, cross_own), halves, 7 * unit
    )
    img_own, img_sent, txt_own, txt_sent = call(
        far_kernel,
        (own_shape, sent_shape, own_shape, sent_shape),
        scalars,
        (own, far, mate_far, cross_far, img_acc, txt_acc),
        halves,
        4 * unit,
    )
    img_back = lax.ppermute(img_sent, AXES, to_img)
    txt_back = lax.ppermute(txt_sent, AXES, to_txt)
    img_grad = call(grad_kernel, sent_shape, (), (img_raw, img_own, img_back))
    txt_grad = call(grad_kernel, sent_shape, (), (txt_raw, txt_own, txt_back))
    return (img_grad, txt_grad)


def solution(mesh):
    moves = routes(mesh.shape["dp"], mesh.shape["fsdp"])
    in_specs = (P(AXES, None), P(AXES, None), P(), P())
    out_specs = (P(AXES, None), P(AXES, None))

    def step(*args):
        return local(*args, moves)

    return jax.shard_map(step, mesh=mesh, in_specs=in_specs, out_specs=out_specs, check_vma=False)
```

```python
import jax
import jax.numpy as jnp
from jax import lax
from jax.experimental import pallas as pl
from jax.experimental.pallas import tpu as pltpu
from jax.sharding import PartitionSpec as P

AXES = ("dp", "fsdp")
SPAN = 16
STRIP = 32
VMEM_LIMIT = 32 * 1024 * 1024


def device_of(block, role, blocks, ways):
    block = block % blocks
    return block * ways + (role + block // SPAN) % ways


def routes(blocks, ways):
    first, second, mate, cross = [], [], [], []
    for block in range(blocks):
        for role in range(ways):
            here = device_of(block, role, blocks, ways)
            img = device_of(block, role ^ 1, blocks, ways)
            txt = device_of(block, ways - 1 - role, blocks, ways)
            across = block + 1 if block % 2 else block - 1
            first.append((here, txt if block % 2 else img))
            second.append((here, img if block % 2 else txt))
            mate.append((here, device_of(block ^ 1, role, blocks, ways)))
            cross.append((here, device_of(across, role, blocks, ways)))
    return first, second, mate, cross


def strips(rows):
    return [slice(start, start + STRIP) for start in range(0, rows, STRIP)]


def inverse_of(values):
    return lax.rsqrt(jnp.sum(values * values, axis=-1, keepdims=True) + 1e-06)


def low_of(raw):
    values = raw.astype(jnp.float32)
    return (values * inverse_of(values)).astype(jnp.bfloat16)


def start_kernel(odd_ref, img_ref, txt_ref, x_raw, y_raw, x_low, y_low, both):
    rows = img_ref.shape[0]
    odd = odd_ref[0] > 0
    for here in strips(rows):
        img, txt = img_ref[here, :], txt_ref[here, :]
        x, y = jnp.where(odd, txt, img), jnp.where(odd, img, txt)
        x_raw[here, :] = x
        y_raw[here, :] = y
        x_low[here, :] = low_of(x)
        y_low[here, :] = low_of(y)
    both[:rows, :] = x_low[...]
    both[rows:, :] = y_low[...]


def scores_of(left, right):
    return lax.dot_general(left, right, (((1,), (1,)), ((), ())), preferred_element_type=jnp.float32)


def negative_coef(left, right, scale, bias):
    return (jax.nn.sigmoid(scale * scores_of(left, right) + bias) * scale).astype(jnp.bfloat16)


def columns_of(width, step=256):
    return [slice(start, start + step) for start in range(0, width, step)]


def dot(coef, rows):
    return jnp.dot(coef, rows, preferred_element_type=jnp.float32)


def stack(out_ref, *pieces):
    rows = out_ref.shape[0] // len(pieces)
    for place, piece in enumerate(pieces):
        out_ref[place * rows : (place + 1) * rows, :] = piece


def side_kernel(scale_ref, bias_ref, own, far, mate, cross, mate_far, cross_far, acc, x, near):
    rows = own.shape[0]
    stack(x, own[...], far[...])
    stack(near, mate[:rows, :], mate_far[...], cross[:rows, :], cross_far[...])
    coef = negative_coef(x[...], near[...], scale_ref[0], bias_ref[0])
    for cols in columns_of(own.shape[1]):
        acc[:, cols] = dot(coef, near[:, cols])


def block_kernel(scale_ref, bias_ref, x_own, x_far, y_own, y_far, acc, kept, sent, coef_t, x, y):
    rows = x_own.shape[0]
    scale, bias = scale_ref[0], bias_ref[0]
    stack(x, x_own[...], x_far[...])
    stack(y, y_own[...], y_far[...])
    shape = (2 * rows, 2 * rows)
    first = lax.broadcasted_iota(jnp.int32, shape, 0)
    positive = (first == lax.broadcasted_iota(jnp.int32, shape, 1)) & (first < rows)
    logits = scale * scores_of(x[...], y[...]) + bias
    size = jax.nn.sigmoid(jnp.where(positive, -logits, logits)) * scale
    signed = jnp.where(positive, -size, size)
    coef = signed.astype(jnp.bfloat16)
    coef_t[...] = signed.T.astype(jnp.bfloat16)
    for cols in columns_of(x_own.shape[1]):
        total = acc[:, cols] + dot(coef, y[:, cols])
        kept[:, cols] = total[:rows]
        sent[:, cols] = total[rows:].astype(jnp.bfloat16)


def last_kernel(
    scale_ref, bias_ref, x_own, x_far, y_own, y_far, coef_t, mate, cross, mate_far, cross_far,
    kept, sent, x, y, near,
):
    rows = x_own.shape[0]
    stack(x, x_own[...], x_far[...])
    stack(y, y_own[...], y_far[...])
    stack(near, mate[rows:, :], mate_far[...], cross[rows:, :], cross_far[...])
    coef = negative_coef(y[...], near[...], scale_ref[0], bias_ref[0])
    for cols in columns_of(x_own.shape[1]):
        total = dot(coef_t[...], x[:, cols]) + dot(coef, near[:, cols])
        kept[:, cols] = total[:rows]
        sent[:, cols] = total[rows:].astype(jnp.bfloat16)


def grad_strip(raw, direction):
    values = raw.astype(jnp.float32)
    inverse = inverse_of(values)
    norm = values * inverse
    inner = jnp.sum(norm * direction, axis=-1, keepdims=True)
    return ((direction - norm * inner) * inverse).astype(jnp.bfloat16)


def first_grad_kernel(raw, kept, there, out):
    for here in strips(raw.shape[0]):
        out[here, :] = grad_strip(raw[here, :], kept[here, :] + there[here, :].astype(jnp.float32))


def second_grad_kernel(odd_ref, raw, kept, there, x_grad, img_grad, txt_grad):
    odd = odd_ref[0] > 0
    for here in strips(raw.shape[0]):
        y = grad_strip(raw[here, :], kept[here, :] + there[here, :].astype(jnp.float32))
        x = x_grad[here, :]
        img_grad[here, :] = jnp.where(odd, y, x)
        txt_grad[here, :] = jnp.where(odd, x, y)


def call(kernel, outs, scalars, arrays, scratch=(), flops=0):
    moved = sum(a.size * a.dtype.itemsize for a in arrays)
    return pl.pallas_call(
        kernel,
        out_shape=outs,
        in_specs=[pl.BlockSpec(memory_space=pltpu.SMEM)] * len(scalars)
        + [pl.BlockSpec(memory_space=pltpu.VMEM)] * len(arrays),
        out_specs=jax.tree.map(lambda _: pl.BlockSpec(memory_space=pltpu.VMEM), outs),
        scratch_shapes=list(scratch),
        compiler_params=pltpu.CompilerParams(vmem_limit_bytes=VMEM_LIMIT),
        cost_estimate=pl.CostEstimate(flops=flops, bytes_accessed=moved, transcendentals=0),
    )(*scalars, *arrays)


def local(img_raw, txt_raw, logit_scale, logit_bias, moves):
    first, second, to_mate, to_cross = moves
    rows, width = img_raw.shape
    odd = (lax.axis_index("dp") % 2).astype(jnp.int32).reshape(1)
    scalars = (logit_scale.reshape(1), logit_bias.reshape(1))

    def shape(count, kind):
        return jax.ShapeDtypeStruct((count * rows, width), kind)

    def space(count):
        return pltpu.VMEM((count * rows, width), jnp.bfloat16)

    piece, kept = shape(1, jnp.bfloat16), shape(1, jnp.float32)
    coef_shape = jax.ShapeDtypeStruct((2 * rows, 2 * rows), jnp.bfloat16)
    unit = 2 * (2 * rows) * (2 * rows) * width

    x_raw, y_raw, x, y, both = call(
        start_kernel, (piece,) * 4 + (shape(2, jnp.bfloat16),), (odd,), (img_raw, txt_raw)
    )
    x_far = lax.ppermute(x, AXES, first)
    y_far = lax.ppermute(y, AXES, second)
    cross = lax.ppermute(both, AXES, to_cross)
    mate = lax.ppermute(both, AXES, to_mate)
    x_cross = lax.ppermute(x_far, AXES, to_cross)
    x_mate = lax.ppermute(x_far, AXES, to_mate)
    acc = call(
        side_kernel,
        shape(2, jnp.float32),
        scalars,
        (x, x_far, mate, cross, x_mate, x_cross),
        (space(2), space(4)),
        4 * unit,
    )
    y_cross = lax.ppermute(y_far, AXES, to_cross)
    y_mate = lax.ppermute(y_far, AXES, to_mate)
    x_kept, x_sent, coef_t = call(
        block_kernel,
        (kept, piece, coef_shape),
        scalars,
        (x, x_far, y, y_far, acc),
        (space(2), space(2)),
        2 * unit,
    )
    x_back = lax.ppermute(x_sent, AXES, first)
    y_kept, y_sent = call(
        last_kernel,
        (kept, piece),
        scalars,
        (x, x_far, y, y_far, coef_t, mate, cross, y_mate, y_cross),
        (space(2), space(2), space(4)),
        5 * unit,
    )
    y_back = lax.ppermute(y_sent, AXES, second)
    x_grad = call(first_grad_kernel, piece, (), (x_raw, x_kept, x_back))
    return call(
        second_grad_kernel, (piece, piece), (odd,), (y_raw, y_kept, y_back, x_grad)
    )


def solution(mesh):
    moves = routes(mesh.shape["dp"], mesh.shape["fsdp"])
    in_specs = (P(AXES, None), P(AXES, None), P(), P())
    out_specs = (P(AXES, None), P(AXES, None))

    def step(*args):
        return local(*args, moves)

    return jax.shard_map(step, mesh=mesh, in_specs=in_specs, out_specs=out_specs, check_vma=False)
```

```python
import jax
import jax.numpy as jnp
from jax import lax
from jax.experimental import pallas as pl
from jax.experimental.pallas import tpu as pltpu
from jax.sharding import PartitionSpec as P

AXES = ("dp", "fsdp")
SPAN = 16
STRIP = 32
VMEM_LIMIT = 16 * 1024 * 1024


def device_of(block, role, blocks, ways):
    block = block % blocks
    return block * ways + (role + block // SPAN) % ways


def routes(blocks, ways):
    first, second, mate, cross = [], [], [], []
    for block in range(blocks):
        for role in range(ways):
            here = device_of(block, role, blocks, ways)
            img = device_of(block, role ^ 1, blocks, ways)
            txt = device_of(block, ways - 1 - role, blocks, ways)
            ahead = device_of(block + 1, role, blocks, ways)
            first.append((here, txt if block % 2 else img))
            second.append((here, img if block % 2 else txt))
            (cross if block % 2 else mate).append((here, ahead))
    return first, second, mate, cross


def swaps(pairs):
    return [*pairs, *((second, first) for first, second in pairs)]


def strips(rows):
    return [slice(start, start + STRIP) for start in range(0, rows, STRIP)]


def inverse_of(values):
    return lax.rsqrt(jnp.sum(values * values, axis=-1, keepdims=True) + 1e-06)


def low_of(raw):
    values = raw.astype(jnp.float32)
    return (values * inverse_of(values)).astype(jnp.bfloat16)


def start_kernel(odd_ref, img_ref, txt_ref, x_low, y_low, both):
    odd = odd_ref[0] > 0
    img, txt = low_of(img_ref[...]), low_of(txt_ref[...])
    x, y = jnp.where(odd, txt, img), jnp.where(odd, img, txt)
    x_low[...] = x
    y_low[...] = y
    both[0] = x
    both[1] = y


def scores_of(left, right):
    return lax.dot_general(left, right, (((1,), (1,)), ((), ())), preferred_element_type=jnp.float32)


def negative_coef(left, right, scale, bias):
    return (jax.nn.sigmoid(scale * scores_of(left, right) + bias) * scale).astype(jnp.bfloat16)


def columns_of(width, step=256):
    return [slice(start, start + step) for start in range(0, width, step)]


def dot(coef, rows):
    return jnp.dot(coef, rows, preferred_element_type=jnp.float32)


def stack(out_ref, *pieces):
    rows = out_ref.shape[0] // len(pieces)
    for place, piece in enumerate(pieces):
        out_ref[place * rows : (place + 1) * rows, :] = piece


def other(ref, place, pieces, piece, rows):
    begin = pl.multiple_of((place * pieces + piece) * rows, rows)
    return ref.at[pl.ds(begin, rows), :]


def fetch(sources, out_ref, sems):
    rows = out_ref.shape[0] // len(sources)
    copies = []
    for place, source in enumerate(sources):
        part = out_ref.at[pl.ds(place * rows, rows), :]
        copies.append(pltpu.make_async_copy(source, part, sems.at[place]))
    for copy in copies:
        copy.start()
    for copy in copies:
        copy.wait()


def near_kernel(
    scale_ref, bias_ref, odd_ref, own, far, mate, cross, acc, y_near, x, near, sems
):
    rows = own.shape[0]
    odd = odd_ref[0]
    stack(x, own[...], far[...])
    places = ((mate, 1 - odd), (cross, odd))
    fetch([other(ref, place, 2, 0, rows) for ref, place in places], near, sems)
    fetch([other(ref, place, 2, 1, rows) for ref, place in places], y_near, sems)
    coef = negative_coef(x[...], near[...], scale_ref[0], bias_ref[0])
    for cols in columns_of(own.shape[1]):
        acc[:, cols] = dot(coef, near[:, cols])


def block_kernel(scale_ref, bias_ref, x_own, x_far, y_own, y_far, acc, out, coef_t, x, y):
    rows = x_own.shape[0]
    scale, bias = scale_ref[0], bias_ref[0]
    stack(x, x_own[...], x_far[...])
    stack(y, y_own[...], y_far[...])
    shape = (2 * rows, 2 * rows)
    first = lax.broadcasted_iota(jnp.int32, shape, 0)
    positive = (first == lax.broadcasted_iota(jnp.int32, shape, 1)) & (first < rows)
    logits = scale * scores_of(x[...], y[...]) + bias
    size = jax.nn.sigmoid(jnp.where(positive, -logits, logits)) * scale
    signed = jnp.where(positive, -size, size)
    coef = signed.astype(jnp.bfloat16)
    coef_t[...] = signed.T.astype(jnp.bfloat16)
    for cols in columns_of(x_own.shape[1]):
        out[:, cols] = acc[:, cols] + dot(coef, y[:, cols])


def far_kernel(
    scale_ref, bias_ref, odd_ref, own, far, acc, mate, cross, kept, sent, side, near, sems
):
    rows = own.shape[0]
    odd = odd_ref[0]
    stack(side, own[...], far[...])
    if mate.shape[0] > rows:
        mate, cross = other(mate, 1 - odd, 1, 0, rows), other(cross, odd, 1, 0, rows)
    fetch([mate, cross], near, sems)
    coef = negative_coef(side[...], near[...], scale_ref[0], bias_ref[0])
    for cols in columns_of(own.shape[1]):
        total = acc[:, cols] + dot(coef, near[:, cols])
        kept[:, cols] = total[:rows]
        sent[:, cols] = total[rows:].astype(jnp.bfloat16)


def far_pass_kernel(
    scale_ref, bias_ref, odd_ref, own, far, acc, held, mate, cross, kept, sent, passed, side, near, sems
):
    passed[...] = held[...]
    far_kernel(
        scale_ref, bias_ref, odd_ref, own, far, acc, mate, cross, kept, sent, side, near, sems
    )


def second_kernel(scale_ref, bias_ref, x_own, x_far, y_own, y_far, coef_t, near, acc, x, y):
    stack(x, x_own[...], x_far[...])
    stack(y, y_own[...], y_far[...])
    coef = negative_coef(y[...], near[...], scale_ref[0], bias_ref[0])
    for cols in columns_of(x_own.shape[1]):
        acc[:, cols] = dot(coef_t[...], x[:, cols]) + dot(coef, near[:, cols])


def grad_strip(raw, direction):
    values = raw.astype(jnp.float32)
    inverse = inverse_of(values)
    norm = values * inverse
    inner = jnp.sum(norm * direction, axis=-1, keepdims=True)
    return ((direction - norm * inner) * inverse).astype(jnp.bfloat16)


def first_grad_kernel(odd_ref, img_raw, txt_raw, kept, there, out):
    odd = odd_ref[0] > 0
    for here in strips(img_raw.shape[0]):
        raw = jnp.where(odd, txt_raw[here, :], img_raw[here, :])
        out[here, :] = grad_strip(raw, kept[here, :] + there[here, :].astype(jnp.float32))


def second_grad_kernel(odd_ref, img_raw, txt_raw, kept, there, x_grad, img_grad, txt_grad):
    odd = odd_ref[0] > 0
    for here in strips(img_raw.shape[0]):
        raw = jnp.where(odd, img_raw[here, :], txt_raw[here, :])
        y = grad_strip(raw, kept[here, :] + there[here, :].astype(jnp.float32))
        x = x_grad[here, :]
        img_grad[here, :] = jnp.where(odd, y, x)
        txt_grad[here, :] = jnp.where(odd, x, y)


def start(odd, img_raw, txt_raw):
    rows, width = img_raw.shape
    strip = pl.BlockSpec((STRIP, width), lambda i: (i, 0))
    piece = jax.ShapeDtypeStruct((rows, width), jnp.bfloat16)
    x, y, both = pl.pallas_call(
        start_kernel,
        grid=(rows // STRIP,),
        out_shape=(piece, piece, jax.ShapeDtypeStruct((2, rows, width), jnp.bfloat16)),
        in_specs=[pl.BlockSpec(memory_space=pltpu.SMEM), strip, strip],
        out_specs=(strip, strip, pl.BlockSpec((2, STRIP, width), lambda i: (0, i, 0))),
        compiler_params=pltpu.CompilerParams(vmem_limit_bytes=VMEM_LIMIT),
    )(odd, img_raw, txt_raw)
    return x, y, both.reshape(2 * rows, width)


def call(kernel, outs, scalars, arrays, there=(), scratch=(), flops=0):
    moved = sum(a.size * a.dtype.itemsize for a in arrays)
    return pl.pallas_call(
        kernel,
        out_shape=outs,
        in_specs=[pl.BlockSpec(memory_space=pltpu.SMEM)] * len(scalars)
        + [pl.BlockSpec(memory_space=pltpu.VMEM)] * len(arrays)
        + [pl.BlockSpec(memory_space=pl.ANY)] * len(there),
        out_specs=jax.tree.map(lambda _: pl.BlockSpec(memory_space=pltpu.VMEM), outs),
        scratch_shapes=list(scratch),
        compiler_params=pltpu.CompilerParams(vmem_limit_bytes=VMEM_LIMIT),
        cost_estimate=pl.CostEstimate(flops=flops, bytes_accessed=moved, transcendentals=0),
    )(*scalars, *arrays, *there)


def local(img_raw, txt_raw, logit_scale, logit_bias, moves):
    first, second, mates, across = moves
    rows, width = img_raw.shape
    odd = (lax.axis_index("dp") & 1).astype(jnp.int32).reshape(1)
    scalars = (logit_scale.reshape(1), logit_bias.reshape(1))

    def shape(count, kind):
        return jax.ShapeDtypeStruct((count * rows, width), kind)

    def gathered(array, groups):
        return lax.all_gather(array, AXES, axis=0, tiled=True, axis_index_groups=[list(group) for group in groups])

    pair, sems = pltpu.VMEM((2 * rows, width), jnp.bfloat16), pltpu.SemaphoreType.DMA((2,))
    piece, kept, acc = shape(1, jnp.bfloat16), shape(1, jnp.float32), shape(2, jnp.float32)
    coef_shape = jax.ShapeDtypeStruct((2 * rows, 2 * rows), jnp.bfloat16)
    unit = 2 * (2 * rows) * (2 * rows) * width

    x, y, both = start(odd, img_raw, txt_raw)
    mate, cross = gathered(both, mates), gathered(both, across)
    x_far = lax.ppermute(x, AXES, first)
    y_far = lax.ppermute(y, AXES, second)
    x_cross = lax.ppermute(x_far, AXES, swaps(across))
    x_mate = lax.ppermute(x_far, AXES, swaps(mates))
    x_acc, y_near = call(
        near_kernel,
        (acc, shape(2, jnp.bfloat16)),
        (*scalars, odd),
        (x, x_far),
        (mate, cross),
        (pair, pair, sems),
        2 * unit,
    )
    x_acc, coef_t = call(
        block_kernel, (acc, coef_shape), scalars, (x, x_far, y, y_far, x_acc), (), (pair, pair), 4 * unit
    )
    x_kept, x_sent, y_passed = call(
        far_pass_kernel,
        (kept, piece, piece),
        (*scalars, odd),
        (x, x_far, x_acc, y_far),
        (x_mate, x_cross),
        (pair, pair, sems),
        2 * unit,
    )
    y_cross, y_mate = gathered(y_passed, across), gathered(y_passed, mates)
    x_back = lax.ppermute(x_sent, AXES, first)
    y_acc = call(
        second_kernel, acc, scalars, (x, x_far, y, y_far, coef_t, y_near), (), (pair, pair), 3 * unit
    )
    y_kept, y_sent = call(
        far_kernel,
        (kept, piece),
        (*scalars, odd),
        (y, y_far, y_acc),
        (y_mate, y_cross),
        (pair, pair, sems),
        2 * unit,
    )
    y_back = lax.ppermute(y_sent, AXES, second)
    x_grad = call(first_grad_kernel, piece, (odd,), (img_raw, txt_raw, x_kept, x_back))
    return call(
        second_grad_kernel,
        (piece, piece),
        (odd,),
        (img_raw, txt_raw, y_kept, y_back, x_grad),
    )


def solution(mesh):
    moves = routes(mesh.shape["dp"], mesh.shape["fsdp"])
    in_specs = (P(AXES, None), P(AXES, None), P(), P())
    out_specs = (P(AXES, None), P(AXES, None))

    def step(*args):
        return local(*args, moves)

    return jax.shard_map(step, mesh=mesh, in_specs=in_specs, out_specs=out_specs, check_vma=False)
```

```python
import jax
import jax.numpy as jnp
from jax import lax
from jax.experimental import pallas as pl
from jax.experimental.pallas import tpu as pltpu
from jax.sharding import PartitionSpec as P

AXES = ("dp", "fsdp")
SPAN = 16
STRIP = 32
VMEM_LIMIT = 32 * 1024 * 1024


def device_of(block, role, blocks, ways):
    block = block % blocks
    return block * ways + (role + block // SPAN) % ways


def routes(blocks, ways):
    img, txt, mate, cross = ([], []), ([], []), [], []
    for block in range(blocks):
        for role in range(ways):
            here = device_of(block, role, blocks, ways)
            across = block + 1 if block % 2 else block - 1
            group = block % SPAN * 2 // SPAN
            img[group].append((here, device_of(block, role ^ 1, blocks, ways)))
            txt[group].append((here, device_of(block, ways - 1 - role, blocks, ways)))
            mate.append((here, device_of(block ^ 1, role, blocks, ways)))
            cross.append((here, device_of(across, role, blocks, ways)))
    return img, txt, mate, cross


def inverse_of(values):
    return lax.rsqrt(jnp.sum(values * values, axis=-1, keepdims=True) + 1e-06)


def low_kernel(img_ref, txt_ref, low_ref):
    rows = img_ref.shape[0]
    for part, ref in enumerate((img_ref, txt_ref)):
        for start in range(0, rows, STRIP):
            values = ref[start : start + STRIP, :].astype(jnp.float32)
            strip = (values * inverse_of(values)).astype(jnp.bfloat16)
            low_ref[part * rows + start : part * rows + start + STRIP, :] = strip


def pass_kernel(img_ref, txt_ref, mate_ref, cross_ref, img_out, txt_out):
    del mate_ref, cross_ref
    img_out[...] = img_ref[...]
    txt_out[...] = txt_ref[...]


def sum_kernel(img_a, img_b, txt_a, txt_b, low_ref):
    rows = img_a.shape[0]
    for part, refs in enumerate(((img_a, img_b), (txt_a, txt_b))):
        for start in range(0, rows, STRIP):
            values = sum(ref[start : start + STRIP, :].astype(jnp.float32) for ref in refs)
            strip = (values * inverse_of(values)).astype(jnp.bfloat16)
            low_ref[part * rows + start : part * rows + start + STRIP, :] = strip


def scores_of(left, right):
    return lax.dot_general(left, right, (((1,), (1,)), ((), ())), preferred_element_type=jnp.float32)


def negative_coef(left, right, scale, bias):
    return (jax.nn.sigmoid(scale * scores_of(left, right) + bias) * scale).astype(jnp.bfloat16)


def columns_of(width, step=256):
    return [slice(start, start + step) for start in range(0, width, step)]


def stack(first, second, part, rows, out_ref):
    out_ref[:rows, :] = first[part * rows : (part + 1) * rows, :]
    out_ref[rows:, :] = second[part * rows : (part + 1) * rows, :]


def near_kernel(scale_ref, bias_ref, own, far, mate, cross, img_acc, txt_acc, img, txt, img_n, txt_n):
    rows = own.shape[0] // 2
    scale, bias = scale_ref[0], bias_ref[0]
    stack(own, far, 0, rows, img)
    stack(own, far, 1, rows, txt)
    stack(mate, cross, 0, rows, img_n)
    stack(mate, cross, 1, rows, txt_n)

    shape = (2 * rows, 2 * rows)
    first = lax.broadcasted_iota(jnp.int32, shape, 0)
    positive = (first == lax.broadcasted_iota(jnp.int32, shape, 1)) & (first < rows)
    logits = scale * scores_of(img[...], txt[...]) + bias
    size = jax.nn.sigmoid(jnp.where(positive, -logits, logits)) * scale
    signed = jnp.where(positive, -size, size)
    coef_own = signed.astype(jnp.bfloat16)
    coef_own_t = signed.T.astype(jnp.bfloat16)
    coef_img = negative_coef(img[...], txt_n[...], scale, bias)
    coef_txt = negative_coef(txt[...], img_n[...], scale, bias)

    def dot(coef, ref, cols):
        return jnp.dot(coef, ref[:, cols], preferred_element_type=jnp.float32)

    for cols in columns_of(own.shape[1]):
        img_acc[:, cols] = dot(coef_own, txt, cols) + dot(coef_img, txt_n, cols)
        txt_acc[:, cols] = dot(coef_own_t, img, cols) + dot(coef_txt, img_n, cols)


def far_kernel(
    scale_ref, bias_ref, own, far, cross, mate, img_acc, txt_acc,
    img_own, img_far, txt_own, txt_far, img, txt, img_n, txt_n,
):
    rows = own.shape[0] // 2
    scale, bias = scale_ref[0], bias_ref[0]
    stack(own, far, 0, rows, img)
    stack(own, far, 1, rows, txt)
    stack(mate, cross, 0, rows, img_n)
    stack(mate, cross, 1, rows, txt_n)
    coef_img = negative_coef(img[...], txt_n[...], scale, bias)
    coef_txt = negative_coef(txt[...], img_n[...], scale, bias)
    for cols in columns_of(own.shape[1]):
        total = img_acc[:, cols] + jnp.dot(
            coef_img, txt_n[:, cols], preferred_element_type=jnp.float32
        )
        img_own[:, cols] = total[:rows]
        img_far[:, cols] = total[rows:].astype(jnp.bfloat16)
        total = txt_acc[:, cols] + jnp.dot(
            coef_txt, img_n[:, cols], preferred_element_type=jnp.float32
        )
        txt_own[:, cols] = total[:rows]
        txt_far[:, cols] = total[rows:].astype(jnp.bfloat16)


def grad_kernel(raw_ref, own_ref, there_ref, out_ref):
    for start in range(0, raw_ref.shape[0], STRIP):
        here = slice(start, start + STRIP)
        values = raw_ref[here, :].astype(jnp.float32)
        inverse = inverse_of(values)
        norm = values * inverse
        direction = own_ref[here, :] + there_ref[here, :].astype(jnp.float32)
        inner = jnp.sum(norm * direction, axis=-1, keepdims=True)
        out_ref[here, :] = ((direction - norm * inner) * inverse).astype(jnp.bfloat16)


def call(kernel, outs, scalars, arrays, there=(), scratch=(), flops=0):
    moved = sum(a.size * a.dtype.itemsize for a in arrays)
    return pl.pallas_call(
        kernel,
        out_shape=outs,
        in_specs=[pl.BlockSpec(memory_space=pltpu.SMEM)] * len(scalars)
        + [pl.BlockSpec(memory_space=pltpu.VMEM)] * len(arrays)
        + [pl.BlockSpec(memory_space=pl.ANY)] * len(there),
        out_specs=jax.tree.map(lambda _: pl.BlockSpec(memory_space=pltpu.VMEM), outs),
        scratch_shapes=list(scratch),
        compiler_params=pltpu.CompilerParams(vmem_limit_bytes=VMEM_LIMIT),
        cost_estimate=pl.CostEstimate(flops=flops, bytes_accessed=moved, transcendentals=0),
    )(*scalars, *arrays, *there)


def local(img_raw, txt_raw, logit_scale, logit_bias, moves):
    to_img, to_txt, to_mate, to_cross = moves
    rows, width = img_raw.shape
    scalars = (logit_scale.reshape(1), logit_bias.reshape(1))
    low_shape = jax.ShapeDtypeStruct((2 * rows, width), jnp.bfloat16)
    acc_shape = jax.ShapeDtypeStruct((2 * rows, width), jnp.float32)
    own_shape = jax.ShapeDtypeStruct((rows, width), jnp.float32)
    sent_shape = jax.ShapeDtypeStruct((rows, width), jnp.bfloat16)
    halves = [pltpu.VMEM((2 * rows, width), jnp.bfloat16)] * 4
    unit = 2 * (2 * rows) * (2 * rows) * width

    img_a = lax.ppermute(img_raw, AXES, to_img[0])
    txt_a = lax.ppermute(txt_raw, AXES, to_txt[0])
    own = call(low_kernel, low_shape, (), (img_raw, txt_raw))
    mate_own = lax.ppermute(own, AXES, to_mate)
    cross_own = lax.ppermute(own, AXES, to_cross)
    img_late, txt_late = call(
        pass_kernel, (sent_shape, sent_shape), (), (img_raw, txt_raw), (mate_own, cross_own)
    )
    img_b = lax.ppermute(img_late, AXES, to_img[1])
    txt_b = lax.ppermute(txt_late, AXES, to_txt[1])
    far = call(sum_kernel, low_shape, (), (img_a, img_b, txt_a, txt_b))
    mate_far = lax.ppermute(far, AXES, to_mate)
    cross_far = lax.ppermute(far, AXES, to_cross)
    img_acc, txt_acc = call(
        near_kernel,
        (acc_shape, acc_shape),
        scalars,
        (own, far, mate_own, cross_own),
        (),
        halves,
        7 * unit,
    )
    img_own, img_sent, txt_own, txt_sent = call(
        far_kernel,
        (own_shape, sent_shape, own_shape, sent_shape),
        scalars,
        (own, far, cross_far, mate_far, img_acc, txt_acc),
        (),
        halves,
        4 * unit,
    )
    img_back = lax.ppermute(img_sent, AXES, to_img[0] + to_img[1])
    txt_back = lax.ppermute(txt_sent, AXES, to_txt[0] + to_txt[1])
    img_grad = call(grad_kernel, sent_shape, (), (img_raw, img_own, img_back))
    txt_grad = call(grad_kernel, sent_shape, (), (txt_raw, txt_own, txt_back))
    return (img_grad, txt_grad)


def solution(mesh):
    moves = routes(mesh.shape["dp"], mesh.shape["fsdp"])
    in_specs = (P(AXES, None), P(AXES, None), P(), P())
    out_specs = (P(AXES, None), P(AXES, None))

    def step(*args):
        return local(*args, moves)

    return jax.shard_map(step, mesh=mesh, in_specs=in_specs, out_specs=out_specs, check_vma=False)
```

```python
import jax
import jax.numpy as jnp
from jax import lax
from jax.experimental import pallas as pl
from jax.experimental.pallas import tpu as pltpu
from jax.sharding import PartitionSpec as P

AXES = ("dp", "fsdp")
SPAN = 16
STRIP = 32
TOKEN = 16
VMEM_LIMIT = 32 * 1024 * 1024


def device_of(block, role, blocks, ways):
    block = block % blocks
    return block * ways + (role + block // SPAN) % ways


def routes(blocks, ways):
    img, txt, mate, cross, token = ([], []), ([], []), [], [], []
    for block in range(blocks):
        for role in range(ways):
            here = device_of(block, role, blocks, ways)
            across = block + 1 if block % 2 else block - 1
            group = block % SPAN * 2 // SPAN
            img[group].append((here, device_of(block, role ^ 1, blocks, ways)))
            txt[group].append((here, device_of(block, ways - 1 - role, blocks, ways)))
            if group == 0:
                token.append((here, device_of(block + SPAN // 2, role, blocks, ways)))
            mate.append((here, device_of(block ^ 1, role, blocks, ways)))
            cross.append((here, device_of(across, role, blocks, ways)))
    return img, txt, mate, cross, token


def inverse_of(values):
    return lax.rsqrt(jnp.sum(values * values, axis=-1, keepdims=True) + 1e-06)


def low_kernel(img_ref, txt_ref, low_ref):
    rows = img_ref.shape[0]
    for part, ref in enumerate((img_ref, txt_ref)):
        for start in range(0, rows, STRIP):
            values = ref[start : start + STRIP, :].astype(jnp.float32)
            strip = (values * inverse_of(values)).astype(jnp.bfloat16)
            low_ref[part * rows + start : part * rows + start + STRIP, :] = strip


def pass_kernel(img_ref, txt_ref, token_ref, img_done, txt_done, img_out, txt_out):
    del token_ref, img_done, txt_done
    img_out[...] = img_ref[...]
    txt_out[...] = txt_ref[...]


def sum_kernel(img_a, img_b, txt_a, txt_b, low_ref):
    rows = img_a.shape[0]
    for part, refs in enumerate(((img_a, img_b), (txt_a, txt_b))):
        for start in range(0, rows, STRIP):
            values = sum(ref[start : start + STRIP, :].astype(jnp.float32) for ref in refs)
            strip = (values * inverse_of(values)).astype(jnp.bfloat16)
            low_ref[part * rows + start : part * rows + start + STRIP, :] = strip


def scores_of(left, right):
    return lax.dot_general(left, right, (((1,), (1,)), ((), ())), preferred_element_type=jnp.float32)


def negative_coef(left, right, scale, bias):
    return (jax.nn.sigmoid(scale * scores_of(left, right) + bias) * scale).astype(jnp.bfloat16)


def columns_of(width, step=256):
    return [slice(start, start + step) for start in range(0, width, step)]


def stack(first, second, part, rows, out_ref):
    out_ref[:rows, :] = first[part * rows : (part + 1) * rows, :]
    out_ref[rows:, :] = second[part * rows : (part + 1) * rows, :]


def near_kernel(scale_ref, bias_ref, own, far, mate, cross, img_acc, txt_acc, img, txt, img_n, txt_n):
    rows = own.shape[0] // 2
    scale, bias = scale_ref[0], bias_ref[0]
    stack(own, far, 0, rows, img)
    stack(own, far, 1, rows, txt)
    stack(mate, cross, 0, rows, img_n)
    stack(mate, cross, 1, rows, txt_n)

    shape = (2 * rows, 2 * rows)
    first = lax.broadcasted_iota(jnp.int32, shape, 0)
    positive = (first == lax.broadcasted_iota(jnp.int32, shape, 1)) & (first < rows)
    logits = scale * scores_of(img[...], txt[...]) + bias
    size = jax.nn.sigmoid(jnp.where(positive, -logits, logits)) * scale
    signed = jnp.where(positive, -size, size)
    coef_own = signed.astype(jnp.bfloat16)
    coef_own_t = signed.T.astype(jnp.bfloat16)
    coef_img = negative_coef(img[...], txt_n[...], scale, bias)
    coef_txt = negative_coef(txt[...], img_n[...], scale, bias)

    def dot(coef, ref, cols):
        return jnp.dot(coef, ref[:, cols], preferred_element_type=jnp.float32)

    for cols in columns_of(own.shape[1]):
        img_acc[:, cols] = dot(coef_own, txt, cols) + dot(coef_img, txt_n, cols)
        txt_acc[:, cols] = dot(coef_own_t, img, cols) + dot(coef_txt, img_n, cols)


def far_kernel(
    scale_ref, bias_ref, own, far, cross, mate, img_acc, txt_acc,
    img_own, img_far, txt_own, txt_far, img, txt, img_n, txt_n,
):
    rows = own.shape[0] // 2
    scale, bias = scale_ref[0], bias_ref[0]
    stack(own, far, 0, rows, img)
    stack(own, far, 1, rows, txt)
    stack(mate, cross, 0, rows, img_n)
    stack(mate, cross, 1, rows, txt_n)
    coef_img = negative_coef(img[...], txt_n[...], scale, bias)
    coef_txt = negative_coef(txt[...], img_n[...], scale, bias)
    for cols in columns_of(own.shape[1]):
        total = img_acc[:, cols] + jnp.dot(
            coef_img, txt_n[:, cols], preferred_element_type=jnp.float32
        )
        img_own[:, cols] = total[:rows]
        img_far[:, cols] = total[rows:].astype(jnp.bfloat16)
        total = txt_acc[:, cols] + jnp.dot(
            coef_txt, img_n[:, cols], preferred_element_type=jnp.float32
        )
        txt_own[:, cols] = total[:rows]
        txt_far[:, cols] = total[rows:].astype(jnp.bfloat16)


def grad_kernel(raw_ref, own_ref, there_ref, out_ref):
    for start in range(0, raw_ref.shape[0], STRIP):
        here = slice(start, start + STRIP)
        values = raw_ref[here, :].astype(jnp.float32)
        inverse = inverse_of(values)
        norm = values * inverse
        direction = own_ref[here, :] + there_ref[here, :].astype(jnp.float32)
        inner = jnp.sum(norm * direction, axis=-1, keepdims=True)
        out_ref[here, :] = ((direction - norm * inner) * inverse).astype(jnp.bfloat16)


def call(kernel, outs, scalars, arrays, there=(), scratch=(), flops=0):
    moved = sum(a.size * a.dtype.itemsize for a in arrays)
    return pl.pallas_call(
        kernel,
        out_shape=outs,
        in_specs=[pl.BlockSpec(memory_space=pltpu.SMEM)] * len(scalars)
        + [pl.BlockSpec(memory_space=pltpu.VMEM)] * len(arrays)
        + [pl.BlockSpec(memory_space=pl.ANY)] * len(there),
        out_specs=jax.tree.map(lambda _: pl.BlockSpec(memory_space=pltpu.VMEM), outs),
        scratch_shapes=list(scratch),
        compiler_params=pltpu.CompilerParams(vmem_limit_bytes=VMEM_LIMIT),
        cost_estimate=pl.CostEstimate(flops=flops, bytes_accessed=moved, transcendentals=0),
    )(*scalars, *arrays, *there)


def local(img_raw, txt_raw, logit_scale, logit_bias, moves):
    to_img, to_txt, to_mate, to_cross, to_late = moves
    rows, width = img_raw.shape
    scalars = (logit_scale.reshape(1), logit_bias.reshape(1))
    low_shape = jax.ShapeDtypeStruct((2 * rows, width), jnp.bfloat16)
    acc_shape = jax.ShapeDtypeStruct((2 * rows, width), jnp.float32)
    own_shape = jax.ShapeDtypeStruct((rows, width), jnp.float32)
    sent_shape = jax.ShapeDtypeStruct((rows, width), jnp.bfloat16)
    halves = [pltpu.VMEM((2 * rows, width), jnp.bfloat16)] * 4
    unit = 2 * (2 * rows) * (2 * rows) * width

    img_a = lax.ppermute(img_raw, AXES, to_img[0])
    txt_a = lax.ppermute(txt_raw, AXES, to_txt[0])
    own = call(low_kernel, low_shape, (), (img_raw, txt_raw))
    mate_own = lax.ppermute(own, AXES, to_mate)
    cross_own = lax.ppermute(own, AXES, to_cross)
    token = lax.ppermute(cross_own[:TOKEN, :128] + mate_own[:TOKEN, :128], AXES, to_late)
    img_late, txt_late = call(
        pass_kernel, (sent_shape, sent_shape), (), (img_raw, txt_raw), (token, img_a, txt_a)
    )
    img_b = lax.ppermute(img_late, AXES, to_img[1])
    txt_b = lax.ppermute(txt_late, AXES, to_txt[1])
    far = call(sum_kernel, low_shape, (), (img_a, img_b, txt_a, txt_b))
    mate_far = lax.ppermute(far, AXES, to_mate)
    cross_far = lax.ppermute(far, AXES, to_cross)
    img_acc, txt_acc = call(
        near_kernel,
        (acc_shape, acc_shape),
        scalars,
        (own, far, mate_own, cross_own),
        (),
        halves,
        7 * unit,
    )
    img_own, img_sent, txt_own, txt_sent = call(
        far_kernel,
        (own_shape, sent_shape, own_shape, sent_shape),
        scalars,
        (own, far, cross_far, mate_far, img_acc, txt_acc),
        (),
        halves,
        4 * unit,
    )
    img_back = lax.ppermute(img_sent, AXES, to_img[0] + to_img[1])
    txt_back = lax.ppermute(txt_sent, AXES, to_txt[0] + to_txt[1])
    img_grad = call(grad_kernel, sent_shape, (), (img_raw, img_own, img_back))
    txt_grad = call(grad_kernel, sent_shape, (), (txt_raw, txt_own, txt_back))
    return (img_grad, txt_grad)


def solution(mesh):
    moves = routes(mesh.shape["dp"], mesh.shape["fsdp"])
    in_specs = (P(AXES, None), P(AXES, None), P(), P())
    out_specs = (P(AXES, None), P(AXES, None))

    def step(*args):
        return local(*args, moves)

    return jax.shard_map(step, mesh=mesh, in_specs=in_specs, out_specs=out_specs, check_vma=False)
```

```python
import jax
import jax.numpy as jnp
from jax import lax
from jax.experimental import pallas as pl
from jax.experimental.pallas import tpu as pltpu
from jax.sharding import PartitionSpec as P

AXES = ("dp", "fsdp")
SPAN = 16
STRIP = 32
VMEM_LIMIT = 16 * 1024 * 1024
PICK_LIMIT = 56 * 1024 * 1024


def device_of(block, role, blocks, ways):
    block = block % blocks
    return block * ways + (role + block // SPAN) % ways


def routes(blocks, ways):
    first, second, mate, cross = [], [], [], []
    for block in range(blocks):
        for role in range(ways):
            here = device_of(block, role, blocks, ways)
            img = device_of(block, role ^ 1, blocks, ways)
            txt = device_of(block, ways - 1 - role, blocks, ways)
            across = block + 1 if block % 2 else block - 1
            first.append((here, txt if block % 2 else img))
            second.append((here, img if block % 2 else txt))
            mate.append((here, device_of(block ^ 1, role, blocks, ways)))
            cross.append((here, device_of(across, role, blocks, ways)))
    return first, second, mate, cross


def inverse_of(values):
    return lax.rsqrt(jnp.sum(values * values, axis=-1, keepdims=True) + 1e-06)


def pick_kernel(odd_ref, img_ref, txt_ref, x_ref, y_ref, sems):
    def move(x_from, y_from):
        copies = [
            pltpu.make_async_copy(x_from, x_ref, sems.at[0]),
            pltpu.make_async_copy(y_from, y_ref, sems.at[1]),
        ]
        for copy in copies:
            copy.start()
        for copy in copies:
            copy.wait()

    @pl.when(odd_ref[0] == 0)
    def _():
        move(img_ref, txt_ref)

    @pl.when(odd_ref[0] != 0)
    def _():
        move(txt_ref, img_ref)


def low_kernel(x_ref, y_ref, low_ref):
    rows = x_ref.shape[0]
    for part, ref in enumerate((x_ref, y_ref)):
        for start in range(0, rows, STRIP):
            values = ref[start : start + STRIP, :].astype(jnp.float32)
            strip = (values * inverse_of(values)).astype(jnp.bfloat16)
            low_ref[part * rows + start : part * rows + start + STRIP, :] = strip


def scores_of(left, right):
    return lax.dot_general(left, right, (((1,), (1,)), ((), ())), preferred_element_type=jnp.float32)


def negative_coef(left, right, scale, bias):
    return (jax.nn.sigmoid(scale * scores_of(left, right) + bias) * scale).astype(jnp.bfloat16)


def columns_of(width, step=256):
    return [slice(start, start + step) for start in range(0, width, step)]


def stack(first, second, part, rows, out_ref):
    out_ref[:rows, :] = first[part * rows : (part + 1) * rows, :]
    out_ref[rows:, :] = second[part * rows : (part + 1) * rows, :]


def near_kernel(scale_ref, bias_ref, own, far, mate, cross, x_acc, y_acc, x, y, x_n, y_n):
    rows = own.shape[0] // 2
    scale, bias = scale_ref[0], bias_ref[0]
    stack(own, far, 0, rows, x)
    stack(own, far, 1, rows, y)
    stack(mate, cross, 0, rows, x_n)
    stack(mate, cross, 1, rows, y_n)

    shape = (2 * rows, 2 * rows)
    first = lax.broadcasted_iota(jnp.int32, shape, 0)
    positive = (first == lax.broadcasted_iota(jnp.int32, shape, 1)) & (first < rows)
    logits = scale * scores_of(x[...], y[...]) + bias
    size = jax.nn.sigmoid(jnp.where(positive, -logits, logits)) * scale
    signed = jnp.where(positive, -size, size)
    coef_own = signed.astype(jnp.bfloat16)
    coef_own_t = signed.T.astype(jnp.bfloat16)
    coef_x = negative_coef(x[...], x_n[...], scale, bias)
    coef_y = negative_coef(y[...], y_n[...], scale, bias)

    def dot(coef, ref, cols):
        return jnp.dot(coef, ref[:, cols], preferred_element_type=jnp.float32)

    for cols in columns_of(own.shape[1]):
        x_acc[:, cols] = dot(coef_own, y, cols) + dot(coef_x, x_n, cols)
        y_acc[:, cols] = dot(coef_own_t, x, cols) + dot(coef_y, y_n, cols)


def far_kernel(
    scale_ref, bias_ref, own, far, mate, cross, x_acc, y_acc,
    x_own, x_far, y_own, y_far, x, y, x_n, y_n,
):
    rows = own.shape[0] // 2
    scale, bias = scale_ref[0], bias_ref[0]
    stack(own, far, 0, rows, x)
    stack(own, far, 1, rows, y)
    stack(mate, cross, 0, rows, x_n)
    stack(mate, cross, 1, rows, y_n)
    coef_x = negative_coef(x[...], x_n[...], scale, bias)
    coef_y = negative_coef(y[...], y_n[...], scale, bias)
    for cols in columns_of(own.shape[1]):
        total = x_acc[:, cols] + jnp.dot(
            coef_x, x_n[:, cols], preferred_element_type=jnp.float32
        )
        x_own[:, cols] = total[:rows]
        x_far[:, cols] = total[rows:].astype(jnp.bfloat16)
        total = y_acc[:, cols] + jnp.dot(
            coef_y, y_n[:, cols], preferred_element_type=jnp.float32
        )
        y_own[:, cols] = total[:rows]
        y_far[:, cols] = total[rows:].astype(jnp.bfloat16)


def grad_strip(raw, direction):
    values = raw.astype(jnp.float32)
    inverse = inverse_of(values)
    norm = values * inverse
    inner = jnp.sum(norm * direction, axis=-1, keepdims=True)
    return ((direction - norm * inner) * inverse).astype(jnp.bfloat16)


def first_grad_kernel(odd_ref, img_raw, txt_raw, kept, there, out):
    odd = odd_ref[0] > 0
    for start in range(0, img_raw.shape[0], STRIP):
        here = slice(start, start + STRIP)
        raw = jnp.where(odd, txt_raw[here, :], img_raw[here, :])
        out[here, :] = grad_strip(raw, kept[here, :] + there[here, :].astype(jnp.float32))


def second_grad_kernel(odd_ref, img_raw, txt_raw, kept, there, x_grad, img_grad, txt_grad):
    odd = odd_ref[0] > 0
    for start in range(0, img_raw.shape[0], STRIP):
        here = slice(start, start + STRIP)
        raw = jnp.where(odd, img_raw[here, :], txt_raw[here, :])
        y = grad_strip(raw, kept[here, :] + there[here, :].astype(jnp.float32))
        x = x_grad[here, :]
        img_grad[here, :] = jnp.where(odd, y, x)
        txt_grad[here, :] = jnp.where(odd, x, y)


def pick(odd, img_raw, txt_raw):
    piece = jax.ShapeDtypeStruct(img_raw.shape, img_raw.dtype)
    return pl.pallas_call(
        pick_kernel,
        out_shape=(piece, piece),
        in_specs=[pl.BlockSpec(memory_space=pltpu.SMEM)] + [pl.BlockSpec(memory_space=pl.ANY)] * 2,
        out_specs=(pl.BlockSpec(memory_space=pltpu.VMEM),) * 2,
        scratch_shapes=[pltpu.SemaphoreType.DMA((2,))],
        compiler_params=pltpu.CompilerParams(vmem_limit_bytes=PICK_LIMIT),
    )(odd, img_raw, txt_raw)


def call(kernel, outs, scalars, arrays, scratch=(), flops=0):
    moved = sum(a.size * a.dtype.itemsize for a in arrays)
    return pl.pallas_call(
        kernel,
        out_shape=outs,
        in_specs=[pl.BlockSpec(memory_space=pltpu.SMEM)] * len(scalars)
        + [pl.BlockSpec(memory_space=pltpu.VMEM)] * len(arrays),
        out_specs=jax.tree.map(lambda _: pl.BlockSpec(memory_space=pltpu.VMEM), outs),
        scratch_shapes=list(scratch),
        compiler_params=pltpu.CompilerParams(vmem_limit_bytes=VMEM_LIMIT),
        cost_estimate=pl.CostEstimate(flops=flops, bytes_accessed=moved, transcendentals=0),
    )(*scalars, *arrays)


def local(img_raw, txt_raw, logit_scale, logit_bias, moves):
    first, second, to_mate, to_cross = moves
    rows, width = img_raw.shape
    odd = (lax.axis_index("dp") & 1).astype(jnp.int32).reshape(1)
    scalars = (logit_scale.reshape(1), logit_bias.reshape(1))
    low_shape = jax.ShapeDtypeStruct((2 * rows, width), jnp.bfloat16)
    acc_shape = jax.ShapeDtypeStruct((2 * rows, width), jnp.float32)
    own_shape = jax.ShapeDtypeStruct((rows, width), jnp.float32)
    sent_shape = jax.ShapeDtypeStruct((rows, width), jnp.bfloat16)
    halves = [pltpu.VMEM((2 * rows, width), jnp.bfloat16)] * 4
    unit = 2 * (2 * rows) * (2 * rows) * width

    x, y = pick(odd, img_raw, txt_raw)
    x_there = lax.ppermute(x, AXES, first)
    y_there = lax.ppermute(y, AXES, second)
    own = call(low_kernel, low_shape, (), (x, y))
    cross_own = lax.ppermute(own, AXES, to_cross)
    mate_own = lax.ppermute(own, AXES, to_mate)
    far = call(low_kernel, low_shape, (), (x_there, y_there))
    cross_far = lax.ppermute(far, AXES, to_cross)
    mate_far = lax.ppermute(far, AXES, to_mate)
    x_acc, y_acc = call(
        near_kernel, (acc_shape, acc_shape), scalars, (own, far, mate_own, cross_own), halves, 7 * unit
    )
    x_kept, x_sent, y_kept, y_sent = call(
        far_kernel,
        (own_shape, sent_shape, own_shape, sent_shape),
        scalars,
        (own, far, mate_far, cross_far, x_acc, y_acc),
        halves,
        4 * unit,
    )
    x_back = lax.ppermute(x_sent, AXES, first)
    y_back = lax.ppermute(y_sent, AXES, second)
    x_grad = call(first_grad_kernel, sent_shape, (odd,), (img_raw, txt_raw, x_kept, x_back))
    return call(
        second_grad_kernel,
        (sent_shape, sent_shape),
        (odd,),
        (img_raw, txt_raw, y_kept, y_back, x_grad),
    )


def solution(mesh):
    moves = routes(mesh.shape["dp"], mesh.shape["fsdp"])
    in_specs = (P(AXES, None), P(AXES, None), P(), P())
    out_specs = (P(AXES, None), P(AXES, None))

    def step(*args):
        return local(*args, moves)

    return jax.shard_map(step, mesh=mesh, in_specs=in_specs, out_specs=out_specs, check_vma=False)
```

```python
import functools

import jax
import jax.numpy as jnp
from jax import lax
from jax.experimental import pallas as pl
from jax.experimental.pallas import tpu as pltpu
from jax.sharding import PartitionSpec as P

AXES = ("dp", "fsdp")
SPAN = 16
STRIP = 32
VMEM_LIMIT = 16 * 1024 * 1024
PIECES = 4
PICK_LIMIT = 56 * 1024 * 1024


def device_of(block, role, blocks, ways):
    block = block % blocks
    return block * ways + (role + block // SPAN) % ways


def routes(blocks, ways):
    first, second, mate, cross = [], [], [], []
    for block in range(blocks):
        for role in range(ways):
            here = device_of(block, role, blocks, ways)
            img = device_of(block, role ^ 1, blocks, ways)
            txt = device_of(block, ways - 1 - role, blocks, ways)
            across = block + 1 if block % 2 else block - 1
            first.append((here, txt if block % 2 else img))
            second.append((here, img if block % 2 else txt))
            mate.append((here, device_of(block ^ 1, role, blocks, ways)))
            cross.append((here, device_of(across, role, blocks, ways)))
    return first, second, mate, cross


def inverse_of(values):
    return lax.rsqrt(jnp.sum(values * values, axis=-1, keepdims=True) + 1e-06)


def pick_kernel(odd_ref, img_ref, txt_ref, x_ref, y_ref, sems):
    def move(x_from, y_from):
        copies = []
        rows = x_ref.shape[0] // PIECES
        for place in range(PIECES):
            here = pl.ds(place * rows, rows)
            for side, (source, out) in enumerate(((x_from, x_ref), (y_from, y_ref))):
                sem = sems.at[side, place]
                copies.append(pltpu.make_async_copy(source.at[here, :], out.at[here, :], sem))
        for copy in copies:
            copy.start()
        for copy in copies:
            copy.wait()

    @pl.when(odd_ref[0] == 0)
    def _():
        move(img_ref, txt_ref)

    @pl.when(odd_ref[0] != 0)
    def _():
        move(txt_ref, img_ref)


def low_kernel(x_ref, y_ref, low_ref):
    rows = x_ref.shape[0]
    for part, ref in enumerate((x_ref, y_ref)):
        for start in range(0, rows, STRIP):
            values = ref[start : start + STRIP, :].astype(jnp.float32)
            strip = (values * inverse_of(values)).astype(jnp.bfloat16)
            low_ref[part * rows + start : part * rows + start + STRIP, :] = strip


def split_low_kernel(x_ref, y_ref, low_ref, x_low, y_low):
    rows = x_ref.shape[0]
    low_kernel(x_ref, y_ref, low_ref)
    x_low[...] = low_ref[:rows, :]
    y_low[...] = low_ref[rows:, :]


def scores_of(left, right):
    return lax.dot_general(left, right, (((1,), (1,)), ((), ())), preferred_element_type=jnp.float32)


def negative_coef(left, right, scale, bias):
    return (jax.nn.sigmoid(scale * scores_of(left, right) + bias) * scale).astype(jnp.bfloat16)


def columns_of(width, step=256):
    return [slice(start, start + step) for start in range(0, width, step)]


def dot(coef, rows):
    return jnp.dot(coef, rows, preferred_element_type=jnp.float32)


def stack(out_ref, first, second):
    rows = first.shape[0]
    out_ref[:rows, :] = first
    out_ref[rows:, :] = second


def half(ref, part):
    rows = ref.shape[0] // 2
    return ref[part * rows : (part + 1) * rows, :]


def near_x_kernel(scale_ref, bias_ref, own, far, mate, cross, acc, coef_t, x, y, near):
    rows = own.shape[0] // 2
    scale, bias = scale_ref[0], bias_ref[0]
    stack(x, half(own, 0), half(far, 0))
    stack(y, half(own, 1), half(far, 1))
    stack(near, half(mate, 0), half(cross, 0))
    shape = (2 * rows, 2 * rows)
    first = lax.broadcasted_iota(jnp.int32, shape, 0)
    positive = (first == lax.broadcasted_iota(jnp.int32, shape, 1)) & (first < rows)
    logits = scale * scores_of(x[...], y[...]) + bias
    size = jax.nn.sigmoid(jnp.where(positive, -logits, logits)) * scale
    signed = jnp.where(positive, -size, size)
    coef_own = signed.astype(jnp.bfloat16)
    coef_t[...] = signed.T.astype(jnp.bfloat16)
    coef = negative_coef(x[...], near[...], scale, bias)
    for cols in columns_of(own.shape[1]):
        acc[:, cols] = dot(coef_own, y[:, cols]) + dot(coef, near[:, cols])


def near_y_kernel(scale_ref, bias_ref, own, far, mate, cross, coef_t, acc, x, y, near):
    stack(x, half(own, 0), half(far, 0))
    stack(y, half(own, 1), half(far, 1))
    stack(near, half(mate, 1), half(cross, 1))
    coef = negative_coef(y[...], near[...], scale_ref[0], bias_ref[0])
    for cols in columns_of(own.shape[1]):
        acc[:, cols] = dot(coef_t[...], x[:, cols]) + dot(coef, near[:, cols])


def far_kernel(part, scale_ref, bias_ref, own, far, cross, mate, acc, kept, sent, side, near):
    rows = own.shape[0] // 2
    stack(side, half(own, part), half(far, part))
    stack(near, half(mate, part), cross[...])
    coef = negative_coef(side[...], near[...], scale_ref[0], bias_ref[0])
    for cols in columns_of(own.shape[1]):
        total = acc[:, cols] + dot(coef, near[:, cols])
        kept[:, cols] = total[:rows]
        sent[:, cols] = total[rows:].astype(jnp.bfloat16)


def far_x_kernel(scale_ref, bias_ref, own, far, cross, mate, acc, coef, kept, sent, passed, *scratch):
    passed[...] = coef[...]
    far_kernel(0, scale_ref, bias_ref, own, far, cross, mate, acc, kept, sent, *scratch)


def grad_strip(raw, direction):
    values = raw.astype(jnp.float32)
    inverse = inverse_of(values)
    norm = values * inverse
    inner = jnp.sum(norm * direction, axis=-1, keepdims=True)
    return ((direction - norm * inner) * inverse).astype(jnp.bfloat16)


def first_grad_kernel(odd_ref, img_raw, txt_raw, kept, there, out):
    odd = odd_ref[0] > 0
    for start in range(0, img_raw.shape[0], STRIP):
        here = slice(start, start + STRIP)
        raw = jnp.where(odd, txt_raw[here, :], img_raw[here, :])
        out[here, :] = grad_strip(raw, kept[here, :] + there[here, :].astype(jnp.float32))


def second_grad_kernel(odd_ref, img_raw, txt_raw, kept, there, x_grad, img_grad, txt_grad):
    odd = odd_ref[0] > 0
    for start in range(0, img_raw.shape[0], STRIP):
        here = slice(start, start + STRIP)
        raw = jnp.where(odd, img_raw[here, :], txt_raw[here, :])
        y = grad_strip(raw, kept[here, :] + there[here, :].astype(jnp.float32))
        x = x_grad[here, :]
        img_grad[here, :] = jnp.where(odd, y, x)
        txt_grad[here, :] = jnp.where(odd, x, y)


def pick(odd, img_raw, txt_raw):
    piece = jax.ShapeDtypeStruct(img_raw.shape, img_raw.dtype)
    return pl.pallas_call(
        pick_kernel,
        out_shape=(piece, piece),
        in_specs=[pl.BlockSpec(memory_space=pltpu.SMEM)] + [pl.BlockSpec(memory_space=pl.ANY)] * 2,
        out_specs=(pl.BlockSpec(memory_space=pltpu.VMEM),) * 2,
        scratch_shapes=[pltpu.SemaphoreType.DMA((2, PIECES))],
        compiler_params=pltpu.CompilerParams(vmem_limit_bytes=PICK_LIMIT),
    )(odd, img_raw, txt_raw)


def call(kernel, outs, scalars, arrays, scratch=(), flops=0):
    moved = sum(a.size * a.dtype.itemsize for a in arrays)
    return pl.pallas_call(
        kernel,
        out_shape=outs,
        in_specs=[pl.BlockSpec(memory_space=pltpu.SMEM)] * len(scalars)
        + [pl.BlockSpec(memory_space=pltpu.VMEM)] * len(arrays),
        out_specs=jax.tree.map(lambda _: pl.BlockSpec(memory_space=pltpu.VMEM), outs),
        scratch_shapes=list(scratch),
        compiler_params=pltpu.CompilerParams(vmem_limit_bytes=VMEM_LIMIT),
        cost_estimate=pl.CostEstimate(flops=flops, bytes_accessed=moved, transcendentals=0),
    )(*scalars, *arrays)


def local(img_raw, txt_raw, logit_scale, logit_bias, moves):
    first, second, to_mate, to_cross = moves
    rows, width = img_raw.shape
    odd = (lax.axis_index("dp") & 1).astype(jnp.int32).reshape(1)
    scalars = (logit_scale.reshape(1), logit_bias.reshape(1))
    low_shape = jax.ShapeDtypeStruct((2 * rows, width), jnp.bfloat16)
    acc_shape = jax.ShapeDtypeStruct((2 * rows, width), jnp.float32)
    own_shape = jax.ShapeDtypeStruct((rows, width), jnp.float32)
    sent_shape = jax.ShapeDtypeStruct((rows, width), jnp.bfloat16)
    coef_shape = jax.ShapeDtypeStruct((2 * rows, 2 * rows), jnp.bfloat16)
    pair = pltpu.VMEM((2 * rows, width), jnp.bfloat16)
    unit = 2 * (2 * rows) * (2 * rows) * width

    x, y = pick(odd, img_raw, txt_raw)
    x_there = lax.ppermute(x, AXES, first)
    y_there = lax.ppermute(y, AXES, second)
    own = call(low_kernel, low_shape, (), (x, y))
    cross_own = lax.ppermute(own, AXES, to_cross)
    mate_own = lax.ppermute(own, AXES, to_mate)
    far, x_far, y_far = call(
        split_low_kernel, (low_shape, sent_shape, sent_shape), (), (x_there, y_there)
    )
    x_cross = lax.ppermute(x_far, AXES, to_cross)
    mate_far = lax.ppermute(far, AXES, to_mate)
    y_cross = lax.ppermute(y_far, AXES, to_cross)
    x_acc, coef_t = call(
        near_x_kernel,
        (acc_shape, coef_shape),
        scalars,
        (own, far, mate_own, cross_own),
        [pair] * 3,
        4 * unit,
    )
    x_kept, x_sent, coef_t = call(
        far_x_kernel,
        (own_shape, sent_shape, coef_shape),
        scalars,
        (own, far, x_cross, mate_far, x_acc, coef_t),
        [pair] * 2,
        2 * unit,
    )
    y_acc = call(
        near_y_kernel,
        acc_shape,
        scalars,
        (own, far, mate_own, cross_own, coef_t),
        [pair] * 3,
        3 * unit,
    )
    y_kept, y_sent = call(
        functools.partial(far_kernel, 1),
        (own_shape, sent_shape),
        scalars,
        (own, far, y_cross, mate_far, y_acc),
        [pair] * 2,
        2 * unit,
    )
    x_back = lax.ppermute(x_sent, AXES, first)
    y_back = lax.ppermute(y_sent, AXES, second)
    x_grad = call(first_grad_kernel, sent_shape, (odd,), (img_raw, txt_raw, x_kept, x_back))
    return call(
        second_grad_kernel,
        (sent_shape, sent_shape),
        (odd,),
        (img_raw, txt_raw, y_kept, y_back, x_grad),
    )


def solution(mesh):
    moves = routes(mesh.shape["dp"], mesh.shape["fsdp"])
    in_specs = (P(AXES, None), P(AXES, None), P(), P())
    out_specs = (P(AXES, None), P(AXES, None))

    def step(*args):
        return local(*args, moves)

    return jax.shard_map(step, mesh=mesh, in_specs=in_specs, out_specs=out_specs, check_vma=False)
```

```python
import functools

import jax
import jax.numpy as jnp
from jax import lax
from jax.experimental import pallas as pl
from jax.experimental.pallas import tpu as pltpu
from jax.sharding import PartitionSpec as P

AXES = ("dp", "fsdp")
SPAN = 16
STRIP = 32
VMEM_LIMIT = 16 * 1024 * 1024
PIECES = 4
PICK_LIMIT = 56 * 1024 * 1024


def device_of(block, role, blocks, ways):
    block = block % blocks
    return block * ways + (role + block // SPAN) % ways


def routes(blocks, ways):
    first, second, mate, cross = [], [], [], []
    for block in range(blocks):
        for role in range(ways):
            here = device_of(block, role, blocks, ways)
            img = device_of(block, role ^ 1, blocks, ways)
            txt = device_of(block, ways - 1 - role, blocks, ways)
            across = block + 1 if block % 2 else block - 1
            first.append((here, txt if block % 2 else img))
            second.append((here, img if block % 2 else txt))
            mate.append((here, device_of(block ^ 1, role, blocks, ways)))
            cross.append((here, device_of(across, role, blocks, ways)))
    return first, second, mate, cross


def inverse_of(values):
    return lax.rsqrt(jnp.sum(values * values, axis=-1, keepdims=True) + 1e-06)


def pick_kernel(odd_ref, img_ref, txt_ref, x_ref, y_ref, sems):
    def move(x_from, y_from):
        copies = []
        rows = x_ref.shape[0] // PIECES
        for place in range(PIECES):
            here = pl.ds(place * rows, rows)
            for side, (source, out) in enumerate(((x_from, x_ref), (y_from, y_ref))):
                sem = sems.at[side, place]
                copies.append(pltpu.make_async_copy(source.at[here, :], out.at[here, :], sem))
        for copy in copies:
            copy.start()
        for copy in copies:
            copy.wait()

    @pl.when(odd_ref[0] == 0)
    def _():
        move(img_ref, txt_ref)

    @pl.when(odd_ref[0] != 0)
    def _():
        move(txt_ref, img_ref)


def low_kernel(x_ref, y_ref, low_ref):
    rows = x_ref.shape[0]
    for part, ref in enumerate((x_ref, y_ref)):
        for start in range(0, rows, STRIP):
            values = ref[start : start + STRIP, :].astype(jnp.float32)
            strip = (values * inverse_of(values)).astype(jnp.bfloat16)
            low_ref[part * rows + start : part * rows + start + STRIP, :] = strip


def split_low_kernel(x_ref, y_ref, low_ref, x_low, y_low):
    rows = x_ref.shape[0]
    low_kernel(x_ref, y_ref, low_ref)
    x_low[...] = low_ref[:rows, :]
    y_low[...] = low_ref[rows:, :]


def scores_of(left, right):
    return lax.dot_general(left, right, (((1,), (1,)), ((), ())), preferred_element_type=jnp.float32)


def negative_coef(left, right, scale, bias):
    return (jax.nn.sigmoid(scale * scores_of(left, right) + bias) * scale).astype(jnp.bfloat16)


def columns_of(width, step=256):
    return [slice(start, start + step) for start in range(0, width, step)]


def dot(coef, rows):
    return jnp.dot(coef, rows, preferred_element_type=jnp.float32)


def stack(out_ref, first, second):
    rows = first.shape[0]
    out_ref[:rows, :] = first
    out_ref[rows:, :] = second


def half(ref, part):
    rows = ref.shape[0] // 2
    return ref[part * rows : (part + 1) * rows, :]


def near_x_kernel(scale_ref, bias_ref, own, far, mate, cross, acc, coef_t, x, y, near):
    rows = own.shape[0] // 2
    scale, bias = scale_ref[0], bias_ref[0]
    stack(x, half(own, 0), half(far, 0))
    stack(y, half(own, 1), half(far, 1))
    stack(near, half(mate, 0), half(cross, 0))
    shape = (2 * rows, 2 * rows)
    first = lax.broadcasted_iota(jnp.int32, shape, 0)
    positive = (first == lax.broadcasted_iota(jnp.int32, shape, 1)) & (first < rows)
    logits = scale * scores_of(x[...], y[...]) + bias
    size = jax.nn.sigmoid(jnp.where(positive, -logits, logits)) * scale
    signed = jnp.where(positive, -size, size)
    coef_own = signed.astype(jnp.bfloat16)
    coef_t[...] = signed.T.astype(jnp.bfloat16)
    coef = negative_coef(x[...], near[...], scale, bias)
    for cols in columns_of(own.shape[1]):
        acc[:, cols] = dot(coef_own, y[:, cols]) + dot(coef, near[:, cols])


def near_y_kernel(scale_ref, bias_ref, own, far, mate, cross, coef_t, after, acc, x, y, near):
    del after
    stack(x, half(own, 0), half(far, 0))
    stack(y, half(own, 1), half(far, 1))
    stack(near, half(mate, 1), half(cross, 1))
    coef = negative_coef(y[...], near[...], scale_ref[0], bias_ref[0])
    for cols in columns_of(own.shape[1]):
        acc[:, cols] = dot(coef_t[...], x[:, cols]) + dot(coef, near[:, cols])


def far_kernel(part, scale_ref, bias_ref, own, far, cross, mate, acc, kept, sent, side, near):
    rows = own.shape[0] // 2
    stack(side, half(own, part), half(far, part))
    stack(near, half(mate, part), cross[...])
    coef = negative_coef(side[...], near[...], scale_ref[0], bias_ref[0])
    for cols in columns_of(own.shape[1]):
        total = acc[:, cols] + dot(coef, near[:, cols])
        kept[:, cols] = total[:rows]
        sent[:, cols] = total[rows:].astype(jnp.bfloat16)


def grad_strip(raw, direction):
    values = raw.astype(jnp.float32)
    inverse = inverse_of(values)
    norm = values * inverse
    inner = jnp.sum(norm * direction, axis=-1, keepdims=True)
    return ((direction - norm * inner) * inverse).astype(jnp.bfloat16)


def first_grad_kernel(odd_ref, img_raw, txt_raw, kept, there, out):
    odd = odd_ref[0] > 0
    for start in range(0, img_raw.shape[0], STRIP):
        here = slice(start, start + STRIP)
        raw = jnp.where(odd, txt_raw[here, :], img_raw[here, :])
        out[here, :] = grad_strip(raw, kept[here, :] + there[here, :].astype(jnp.float32))


def second_grad_kernel(odd_ref, img_raw, txt_raw, kept, there, x_grad, img_grad, txt_grad):
    odd = odd_ref[0] > 0
    for start in range(0, img_raw.shape[0], STRIP):
        here = slice(start, start + STRIP)
        raw = jnp.where(odd, img_raw[here, :], txt_raw[here, :])
        y = grad_strip(raw, kept[here, :] + there[here, :].astype(jnp.float32))
        x = x_grad[here, :]
        img_grad[here, :] = jnp.where(odd, y, x)
        txt_grad[here, :] = jnp.where(odd, x, y)


def pick(odd, img_raw, txt_raw):
    piece = jax.ShapeDtypeStruct(img_raw.shape, img_raw.dtype)
    return pl.pallas_call(
        pick_kernel,
        out_shape=(piece, piece),
        in_specs=[pl.BlockSpec(memory_space=pltpu.SMEM)] + [pl.BlockSpec(memory_space=pl.ANY)] * 2,
        out_specs=(pl.BlockSpec(memory_space=pl.ANY),) * 2,
        scratch_shapes=[pltpu.SemaphoreType.DMA((2, PIECES))],
        compiler_params=pltpu.CompilerParams(vmem_limit_bytes=PICK_LIMIT),
    )(odd, img_raw, txt_raw)


def call(kernel, outs, scalars, arrays, scratch=(), flops=0, there=()):
    moved = sum(a.size * a.dtype.itemsize for a in arrays)
    return pl.pallas_call(
        kernel,
        out_shape=outs,
        in_specs=[pl.BlockSpec(memory_space=pltpu.SMEM)] * len(scalars)
        + [pl.BlockSpec(memory_space=pltpu.VMEM)] * len(arrays)
        + [pl.BlockSpec(memory_space=pl.ANY)] * len(there),
        out_specs=jax.tree.map(lambda _: pl.BlockSpec(memory_space=pltpu.VMEM), outs),
        scratch_shapes=list(scratch),
        compiler_params=pltpu.CompilerParams(vmem_limit_bytes=VMEM_LIMIT),
        cost_estimate=pl.CostEstimate(flops=flops, bytes_accessed=moved, transcendentals=0),
    )(*scalars, *arrays, *there)


def local(img_raw, txt_raw, logit_scale, logit_bias, moves):
    first, second, to_mate, to_cross = moves
    rows, width = img_raw.shape
    odd = (lax.axis_index("dp") & 1).astype(jnp.int32).reshape(1)
    scalars = (logit_scale.reshape(1), logit_bias.reshape(1))
    low_shape = jax.ShapeDtypeStruct((2 * rows, width), jnp.bfloat16)
    acc_shape = jax.ShapeDtypeStruct((2 * rows, width), jnp.float32)
    own_shape = jax.ShapeDtypeStruct((rows, width), jnp.float32)
    sent_shape = jax.ShapeDtypeStruct((rows, width), jnp.bfloat16)
    coef_shape = jax.ShapeDtypeStruct((2 * rows, 2 * rows), jnp.bfloat16)
    pair = pltpu.VMEM((2 * rows, width), jnp.bfloat16)
    unit = 2 * (2 * rows) * (2 * rows) * width

    x, y = pick(odd, img_raw, txt_raw)
    x_there = lax.ppermute(x, AXES, first)
    y_there = lax.ppermute(y, AXES, second)
    own = call(low_kernel, low_shape, (), (x, y))
    cross_own = lax.ppermute(own, AXES, to_cross)
    mate_own = lax.ppermute(own, AXES, to_mate)
    far, x_far, y_far = call(
        split_low_kernel, (low_shape, sent_shape, sent_shape), (), (x_there, y_there)
    )
    x_cross = lax.ppermute(x_far, AXES, to_cross)
    mate_far = lax.ppermute(far, AXES, to_mate)
    y_cross = lax.ppermute(y_far, AXES, to_cross)
    x_acc, coef_t = call(
        near_x_kernel,
        (acc_shape, coef_shape),
        scalars,
        (own, far, mate_own, cross_own),
        [pair] * 3,
        4 * unit,
    )
    x_kept, x_sent = call(
        functools.partial(far_kernel, 0),
        (own_shape, sent_shape),
        scalars,
        (own, far, x_cross, mate_far, x_acc),
        [pair] * 2,
        2 * unit,
    )
    y_acc = call(
        near_y_kernel,
        acc_shape,
        scalars,
        (own, far, mate_own, cross_own, coef_t),
        [pair] * 3,
        3 * unit,
        (x_sent,),
    )
    y_kept, y_sent = call(
        functools.partial(far_kernel, 1),
        (own_shape, sent_shape),
        scalars,
        (own, far, y_cross, mate_far, y_acc),
        [pair] * 2,
        2 * unit,
    )
    x_back = lax.ppermute(x_sent, AXES, first)
    y_back = lax.ppermute(y_sent, AXES, second)
    x_grad = call(first_grad_kernel, sent_shape, (odd,), (img_raw, txt_raw, x_kept, x_back))
    return call(
        second_grad_kernel,
        (sent_shape, sent_shape),
        (odd,),
        (img_raw, txt_raw, y_kept, y_back, x_grad),
    )


def solution(mesh):
    moves = routes(mesh.shape["dp"], mesh.shape["fsdp"])
    in_specs = (P(AXES, None), P(AXES, None), P(), P())
    out_specs = (P(AXES, None), P(AXES, None))

    def step(*args):
        return local(*args, moves)

    return jax.shard_map(step, mesh=mesh, in_specs=in_specs, out_specs=out_specs, check_vma=False)
```

```python
import functools

import jax
import jax.numpy as jnp
from jax import lax
from jax.experimental import pallas as pl
from jax.experimental.pallas import tpu as pltpu
from jax.sharding import PartitionSpec as P

AXES = ("dp", "fsdp")
SPAN = 16
STRIP = 32
VMEM_LIMIT = 16 * 1024 * 1024


def device_of(block, role, blocks, ways):
    block = block % blocks
    return block * ways + (role + block // SPAN) % ways


def routes(blocks, ways):
    first, second, mate, cross = [], [], [], []
    for block in range(blocks):
        for role in range(ways):
            here = device_of(block, role, blocks, ways)
            img = device_of(block, role ^ 1, blocks, ways)
            txt = device_of(block, ways - 1 - role, blocks, ways)
            across = block + 1 if block % 2 else block - 1
            first.append((here, txt if block % 2 else img))
            second.append((here, img if block % 2 else txt))
            mate.append((here, device_of(block ^ 1, role, blocks, ways)))
            cross.append((here, device_of(across, role, blocks, ways)))
    return first, second, mate, cross


def inverse_of(values):
    return lax.rsqrt(jnp.sum(values * values, axis=-1, keepdims=True) + 1e-06)


def low_kernel(x_ref, y_ref, low_ref):
    rows = x_ref.shape[0]
    for part, ref in enumerate((x_ref, y_ref)):
        for start in range(0, rows, STRIP):
            values = ref[start : start + STRIP, :].astype(jnp.float32)
            strip = (values * inverse_of(values)).astype(jnp.bfloat16)
            low_ref[part * rows + start : part * rows + start + STRIP, :] = strip


def split_low_kernel(x_ref, y_ref, low_ref, x_low, y_low):
    rows = x_ref.shape[0]
    low_kernel(x_ref, y_ref, low_ref)
    x_low[...] = low_ref[:rows, :]
    y_low[...] = low_ref[rows:, :]


def scores_of(left, right):
    return lax.dot_general(left, right, (((1,), (1,)), ((), ())), preferred_element_type=jnp.float32)


def negative_coef(left, right, scale, bias):
    return (jax.nn.sigmoid(scale * scores_of(left, right) + bias) * scale).astype(jnp.bfloat16)


def each_columns(width, body, step=256):
    def run(place, carry):
        body(pl.ds(pl.multiple_of(place * step, step), step))
        return carry

    lax.fori_loop(0, width // step, run, 0)


def dot(coef, rows):
    return jnp.dot(coef, rows, preferred_element_type=jnp.float32)


def stack(out_ref, first, second):
    rows = first.shape[0]
    out_ref[:rows, :] = first
    out_ref[rows:, :] = second


def half(ref, part):
    rows = ref.shape[0] // 2
    return ref[part * rows : (part + 1) * rows, :]


def near_x_kernel(scale_ref, bias_ref, own, far, mate, cross, acc, coef_t, x, y, near):
    rows = own.shape[0] // 2
    scale, bias = scale_ref[0], bias_ref[0]
    stack(x, half(own, 0), half(far, 0))
    stack(y, half(own, 1), half(far, 1))
    stack(near, half(mate, 0), half(cross, 0))
    shape = (2 * rows, 2 * rows)
    first = lax.broadcasted_iota(jnp.int32, shape, 0)
    positive = (first == lax.broadcasted_iota(jnp.int32, shape, 1)) & (first < rows)
    logits = scale * scores_of(x[...], y[...]) + bias
    size = jax.nn.sigmoid(jnp.where(positive, -logits, logits)) * scale
    signed = jnp.where(positive, -size, size)
    coef_own = signed.astype(jnp.bfloat16)
    coef_t[...] = signed.T.astype(jnp.bfloat16)
    coef = negative_coef(x[...], near[...], scale, bias)

    def body(cols):
        acc[:, cols] = dot(coef_own, y[:, cols]) + dot(coef, near[:, cols])

    each_columns(own.shape[1], body)


def near_y_kernel(scale_ref, bias_ref, x, y, mate, cross, coef_t, after, acc, near):
    del after
    stack(near, half(mate, 1), half(cross, 1))
    coef = negative_coef(y[...], near[...], scale_ref[0], bias_ref[0])

    def body(cols):
        acc[:, cols] = dot(coef_t[...], x[:, cols]) + dot(coef, near[:, cols])

    each_columns(x.shape[1], body)


def far_kernel(part, scale_ref, bias_ref, side, cross, mate, acc, kept, sent, near):
    rows = kept.shape[0]
    stack(near, half(mate, part), cross[...])
    coef = negative_coef(side[...], near[...], scale_ref[0], bias_ref[0])

    def body(cols):
        total = acc[:, cols] + dot(coef, near[:, cols])
        kept[:, cols] = total[:rows]
        sent[:, cols] = total[rows:].astype(jnp.bfloat16)

    each_columns(side.shape[1], body)


def grad_strip(raw, direction):
    values = raw.astype(jnp.float32)
    inverse = inverse_of(values)
    norm = values * inverse
    inner = jnp.sum(norm * direction, axis=-1, keepdims=True)
    return ((direction - norm * inner) * inverse).astype(jnp.bfloat16)


def first_grad_kernel(odd_ref, img_raw, txt_raw, kept, there, out):
    odd = odd_ref[0] > 0
    for start in range(0, img_raw.shape[0], STRIP):
        here = slice(start, start + STRIP)
        raw = jnp.where(odd, txt_raw[here, :], img_raw[here, :])
        out[here, :] = grad_strip(raw, kept[here, :] + there[here, :].astype(jnp.float32))


def second_grad_kernel(odd_ref, img_raw, txt_raw, kept, there, x_grad, img_grad, txt_grad):
    odd = odd_ref[0] > 0
    for start in range(0, img_raw.shape[0], STRIP):
        here = slice(start, start + STRIP)
        raw = jnp.where(odd, img_raw[here, :], txt_raw[here, :])
        y = grad_strip(raw, kept[here, :] + there[here, :].astype(jnp.float32))
        x = x_grad[here, :]
        img_grad[here, :] = jnp.where(odd, y, x)
        txt_grad[here, :] = jnp.where(odd, x, y)


def call(kernel, outs, scalars, arrays, scratch=(), flops=0, there=()):
    moved = sum(a.size * a.dtype.itemsize for a in arrays)
    return pl.pallas_call(
        kernel,
        out_shape=outs,
        in_specs=[pl.BlockSpec(memory_space=pltpu.SMEM)] * len(scalars)
        + [pl.BlockSpec(memory_space=pltpu.VMEM)] * len(arrays)
        + [pl.BlockSpec(memory_space=pl.ANY)] * len(there),
        out_specs=jax.tree.map(lambda _: pl.BlockSpec(memory_space=pltpu.VMEM), outs),
        scratch_shapes=list(scratch),
        compiler_params=pltpu.CompilerParams(vmem_limit_bytes=VMEM_LIMIT),
        cost_estimate=pl.CostEstimate(flops=flops, bytes_accessed=moved, transcendentals=0),
    )(*scalars, *arrays, *there)


def local(img_raw, txt_raw, logit_scale, logit_bias, moves):
    first, second, to_mate, to_cross = moves
    rows, width = img_raw.shape
    odd = (lax.axis_index("dp") & 1).astype(jnp.int32).reshape(1)
    scalars = (logit_scale.reshape(1), logit_bias.reshape(1))
    low_shape = jax.ShapeDtypeStruct((2 * rows, width), jnp.bfloat16)
    acc_shape = jax.ShapeDtypeStruct((2 * rows, width), jnp.float32)
    own_shape = jax.ShapeDtypeStruct((rows, width), jnp.float32)
    sent_shape = jax.ShapeDtypeStruct((rows, width), jnp.bfloat16)
    coef_shape = jax.ShapeDtypeStruct((2 * rows, 2 * rows), jnp.bfloat16)
    pair = pltpu.VMEM((2 * rows, width), jnp.bfloat16)
    unit = 2 * (2 * rows) * (2 * rows) * width

    x = jnp.where(odd > 0, txt_raw, img_raw)
    y = jnp.where(odd > 0, img_raw, txt_raw)
    x_there = lax.ppermute(x, AXES, first)
    y_there = lax.ppermute(y, AXES, second)
    own = call(low_kernel, low_shape, (), (x, y))
    cross_own = lax.ppermute(own, AXES, to_cross)
    mate_own = lax.ppermute(own, AXES, to_mate)
    far, x_far, y_far = call(
        split_low_kernel, (low_shape, sent_shape, sent_shape), (), (x_there, y_there)
    )
    x_cross = lax.ppermute(x_far, AXES, to_cross)
    mate_far = lax.ppermute(far, AXES, to_mate)
    y_cross = lax.ppermute(y_far, AXES, to_cross)
    x_acc, coef_t, x_half, y_half = call(
        near_x_kernel,
        (acc_shape, coef_shape, low_shape, low_shape),
        scalars,
        (own, far, mate_own, cross_own),
        [pair],
        4 * unit,
    )
    x_kept, x_sent = call(
        functools.partial(far_kernel, 0),
        (own_shape, sent_shape),
        scalars,
        (x_half, x_cross, mate_far, x_acc),
        [pair],
        2 * unit,
    )
    y_acc = call(
        near_y_kernel,
        acc_shape,
        scalars,
        (x_half, y_half, mate_own, cross_own, coef_t),
        [pair],
        3 * unit,
        (x_sent,),
    )
    y_kept, y_sent = call(
        functools.partial(far_kernel, 1),
        (own_shape, sent_shape),
        scalars,
        (y_half, y_cross, mate_far, y_acc),
        [pair],
        2 * unit,
    )
    x_back = lax.ppermute(x_sent, AXES, first)
    y_back = lax.ppermute(y_sent, AXES, second)
    x_grad = call(first_grad_kernel, sent_shape, (odd,), (img_raw, txt_raw, x_kept, x_back))
    return call(
        second_grad_kernel,
        (sent_shape, sent_shape),
        (odd,),
        (img_raw, txt_raw, y_kept, y_back, x_grad),
    )


def solution(mesh):
    moves = routes(mesh.shape["dp"], mesh.shape["fsdp"])
    in_specs = (P(AXES, None), P(AXES, None), P(), P())
    out_specs = (P(AXES, None), P(AXES, None))

    def step(*args):
        return local(*args, moves)

    return jax.shard_map(step, mesh=mesh, in_specs=in_specs, out_specs=out_specs, check_vma=False)
```

```python
import functools

import jax
import jax.numpy as jnp
from jax import lax
from jax.experimental import pallas as pl
from jax.experimental.pallas import tpu as pltpu
from jax.sharding import PartitionSpec as P

AXES = ("dp", "fsdp")
SPAN = 16
STRIP = 32
VMEM_LIMIT = 16 * 1024 * 1024


def device_of(block, role, blocks, ways):
    block = block % blocks
    return block * ways + (role + block // SPAN) % ways


def routes(blocks, ways):
    first, second, mate, cross = [], [], [], []
    for block in range(blocks):
        for role in range(ways):
            here = device_of(block, role, blocks, ways)
            img = device_of(block, role ^ 1, blocks, ways)
            txt = device_of(block, ways - 1 - role, blocks, ways)
            across = block + 1 if block % 2 else block - 1
            first.append((here, txt if block % 2 else img))
            second.append((here, img if block % 2 else txt))
            mate.append((here, device_of(block ^ 1, role, blocks, ways)))
            cross.append((here, device_of(across, role, blocks, ways)))
    return first, second, mate, cross


def inverse_of(values):
    return lax.rsqrt(jnp.sum(values * values, axis=-1, keepdims=True) + 1e-06)


def low_kernel(x_ref, y_ref, low_ref):
    rows = x_ref.shape[0]
    for part, ref in enumerate((x_ref, y_ref)):
        for start in range(0, rows, STRIP):
            values = ref[start : start + STRIP, :].astype(jnp.float32)
            strip = (values * inverse_of(values)).astype(jnp.bfloat16)
            low_ref[part * rows + start : part * rows + start + STRIP, :] = strip


def split_low_kernel(x_ref, y_ref, low_ref, x_low, y_low):
    rows = x_ref.shape[0]
    low_kernel(x_ref, y_ref, low_ref)
    x_low[...] = low_ref[:rows, :]
    y_low[...] = low_ref[rows:, :]


def scores_of(left, right):
    return lax.dot_general(left, right, (((1,), (1,)), ((), ())), preferred_element_type=jnp.float32)


def negative_coef(left, right, scale, bias):
    return (jax.nn.sigmoid(scale * scores_of(left, right) + bias) * scale).astype(jnp.bfloat16)


def each_columns(width, body, step=256):
    for start in range(0, width, step):
        body(slice(start, start + step))


def dot(coef, rows):
    return jnp.dot(coef, rows, preferred_element_type=jnp.float32)


def stack(out_ref, first, second):
    rows = first.shape[0]
    out_ref[:rows, :] = first
    out_ref[rows:, :] = second


def half(ref, part):
    rows = ref.shape[0] // 2
    return ref[part * rows : (part + 1) * rows, :]


def near_x_kernel(scale_ref, bias_ref, own, far, mate, cross, acc, coef_t, x, y, near):
    rows = own.shape[0] // 2
    scale, bias = scale_ref[0], bias_ref[0]
    stack(x, half(own, 0), half(far, 0))
    stack(y, half(own, 1), half(far, 1))
    stack(near, half(mate, 0), half(cross, 0))
    shape = (2 * rows, 2 * rows)
    first = lax.broadcasted_iota(jnp.int32, shape, 0)
    positive = (first == lax.broadcasted_iota(jnp.int32, shape, 1)) & (first < rows)
    logits = scale * scores_of(x[...], y[...]) + bias
    size = jax.nn.sigmoid(jnp.where(positive, -logits, logits)) * scale
    signed = jnp.where(positive, -size, size)
    coef_own = signed.astype(jnp.bfloat16)
    coef_t[...] = signed.T.astype(jnp.bfloat16)
    coef = negative_coef(x[...], near[...], scale, bias)

    def body(cols):
        acc[:, cols] = dot(coef_own, y[:, cols]) + dot(coef, near[:, cols])

    each_columns(own.shape[1], body)


def near_y_kernel(scale_ref, bias_ref, x, y, mate, cross, coef_t, after, acc, near):
    del after
    stack(near, half(mate, 1), half(cross, 1))
    coef = negative_coef(y[...], near[...], scale_ref[0], bias_ref[0])

    def body(cols):
        acc[:, cols] = dot(coef_t[...], x[:, cols]) + dot(coef, near[:, cols])

    each_columns(x.shape[1], body)


def far_kernel(part, scale_ref, bias_ref, side, cross, mate, acc, kept, sent, near):
    rows = kept.shape[0]
    stack(near, half(mate, part), cross[...])
    coef = negative_coef(side[...], near[...], scale_ref[0], bias_ref[0])

    def body(cols):
        total = acc[:, cols] + dot(coef, near[:, cols])
        kept[:, cols] = total[:rows]
        sent[:, cols] = total[rows:].astype(jnp.bfloat16)

    each_columns(side.shape[1], body)


def grad_strip(raw, direction):
    values = raw.astype(jnp.float32)
    inverse = inverse_of(values)
    norm = values * inverse
    inner = jnp.sum(norm * direction, axis=-1, keepdims=True)
    return ((direction - norm * inner) * inverse).astype(jnp.bfloat16)


def first_grad_kernel(odd_ref, img_raw, txt_raw, kept, there, out):
    odd = odd_ref[0] > 0
    for start in range(0, img_raw.shape[0], STRIP):
        here = slice(start, start + STRIP)
        raw = jnp.where(odd, txt_raw[here, :], img_raw[here, :])
        out[here, :] = grad_strip(raw, kept[here, :] + there[here, :].astype(jnp.float32))


def second_grad_kernel(odd_ref, img_raw, txt_raw, kept, there, x_grad, img_grad, txt_grad):
    odd = odd_ref[0] > 0
    for start in range(0, img_raw.shape[0], STRIP):
        here = slice(start, start + STRIP)
        raw = jnp.where(odd, img_raw[here, :], txt_raw[here, :])
        y = grad_strip(raw, kept[here, :] + there[here, :].astype(jnp.float32))
        x = x_grad[here, :]
        img_grad[here, :] = jnp.where(odd, y, x)
        txt_grad[here, :] = jnp.where(odd, x, y)


def call(kernel, outs, scalars, arrays, scratch=(), flops=0, there=()):
    moved = sum(a.size * a.dtype.itemsize for a in arrays)
    return pl.pallas_call(
        kernel,
        out_shape=outs,
        in_specs=[pl.BlockSpec(memory_space=pltpu.SMEM)] * len(scalars)
        + [pl.BlockSpec(memory_space=pltpu.VMEM)] * len(arrays)
        + [pl.BlockSpec(memory_space=pl.ANY)] * len(there),
        out_specs=jax.tree.map(lambda _: pl.BlockSpec(memory_space=pltpu.VMEM), outs),
        scratch_shapes=list(scratch),
        compiler_params=pltpu.CompilerParams(vmem_limit_bytes=VMEM_LIMIT),
        cost_estimate=pl.CostEstimate(flops=flops, bytes_accessed=moved, transcendentals=0),
    )(*scalars, *arrays, *there)


def local(img_raw, txt_raw, logit_scale, logit_bias, moves):
    first, second, to_mate, to_cross = moves
    rows, width = img_raw.shape
    odd = (lax.axis_index("dp") & 1).astype(jnp.int32).reshape(1)
    scalars = (logit_scale.reshape(1), logit_bias.reshape(1))
    low_shape = jax.ShapeDtypeStruct((2 * rows, width), jnp.bfloat16)
    acc_shape = jax.ShapeDtypeStruct((2 * rows, width), jnp.float32)
    own_shape = jax.ShapeDtypeStruct((rows, width), jnp.float32)
    sent_shape = jax.ShapeDtypeStruct((rows, width), jnp.bfloat16)
    coef_shape = jax.ShapeDtypeStruct((2 * rows, 2 * rows), jnp.bfloat16)
    pair = pltpu.VMEM((2 * rows, width), jnp.bfloat16)
    unit = 2 * (2 * rows) * (2 * rows) * width

    x = jnp.where(odd > 0, txt_raw, img_raw)
    y = jnp.where(odd > 0, img_raw, txt_raw)
    x_there = lax.ppermute(x, AXES, first)
    y_there = lax.ppermute(y, AXES, second)
    own = call(low_kernel, low_shape, (), (x, y))
    cross_own = lax.ppermute(own, AXES, to_cross)
    mate_own = lax.ppermute(own, AXES, to_mate)
    far, x_far, y_far = call(
        split_low_kernel, (low_shape, sent_shape, sent_shape), (), (x_there, y_there)
    )
    x_cross = lax.ppermute(x_far, AXES, to_cross)
    mate_far = lax.ppermute(far, AXES, to_mate)
    y_cross = lax.ppermute(y_far, AXES, to_cross)
    x_acc, coef_t, x_half, y_half = call(
        near_x_kernel,
        (acc_shape, coef_shape, low_shape, low_shape),
        scalars,
        (own, far, mate_own, cross_own),
        [pair],
        4 * unit,
    )
    x_kept, x_sent = call(
        functools.partial(far_kernel, 0),
        (own_shape, sent_shape),
        scalars,
        (x_half, x_cross, mate_far, x_acc),
        [pair],
        2 * unit,
    )
    y_acc = call(
        near_y_kernel,
        acc_shape,
        scalars,
        (x_half, y_half, mate_own, cross_own, coef_t),
        [pair],
        3 * unit,
        (x_sent,),
    )
    y_kept, y_sent = call(
        functools.partial(far_kernel, 1),
        (own_shape, sent_shape),
        scalars,
        (y_half, y_cross, mate_far, y_acc),
        [pair],
        2 * unit,
    )
    x_back = lax.ppermute(x_sent, AXES, first)
    y_back = lax.ppermute(y_sent, AXES, second)
    x_grad = call(first_grad_kernel, sent_shape, (odd,), (img_raw, txt_raw, x_kept, x_back))
    return call(
        second_grad_kernel,
        (sent_shape, sent_shape),
        (odd,),
        (img_raw, txt_raw, y_kept, y_back, x_grad),
    )


def solution(mesh):
    moves = routes(mesh.shape["dp"], mesh.shape["fsdp"])
    in_specs = (P(AXES, None), P(AXES, None), P(), P())
    out_specs = (P(AXES, None), P(AXES, None))

    def step(*args):
        return local(*args, moves)

    return jax.shard_map(step, mesh=mesh, in_specs=in_specs, out_specs=out_specs, check_vma=False)
```

```python
import jax
import jax.numpy as jnp
from jax import lax
from jax.experimental import pallas as pl
from jax.experimental.pallas import tpu as pltpu
from jax.sharding import PartitionSpec as P

AXES = ("dp", "fsdp")
SPAN = 16
STRIP = 32
VMEM_LIMIT = 16 * 1024 * 1024


def device_of(block, role, blocks, ways):
    block = block % blocks
    return block * ways + (role + block // SPAN) % ways


def routes(blocks, ways):
    first, second, mate, cross = [], [], [], []
    for block in range(blocks):
        for role in range(ways):
            here = device_of(block, role, blocks, ways)
            img = device_of(block, role ^ 1, blocks, ways)
            txt = device_of(block, ways - 1 - role, blocks, ways)
            across = block + 1 if block % 2 else block - 1
            first.append((here, txt if block % 2 else img))
            second.append((here, img if block % 2 else txt))
            mate.append((here, device_of(block ^ 1, role, blocks, ways)))
            cross.append((here, device_of(across, role, blocks, ways)))
    return first, second, mate, cross


def inverse_of(values):
    return lax.rsqrt(jnp.sum(values * values, axis=-1, keepdims=True) + 1e-06)


def low_kernel(x_ref, y_ref, low_ref):
    rows = x_ref.shape[0]
    for part, ref in enumerate((x_ref, y_ref)):
        for start in range(0, rows, STRIP):
            values = ref[start : start + STRIP, :].astype(jnp.float32)
            strip = (values * inverse_of(values)).astype(jnp.bfloat16)
            low_ref[part * rows + start : part * rows + start + STRIP, :] = strip


def one_low_kernel(raw_ref, low_ref):
    for start in range(0, raw_ref.shape[0], STRIP):
        here = slice(start, start + STRIP)
        values = raw_ref[here, :].astype(jnp.float32)
        low_ref[here, :] = (values * inverse_of(values)).astype(jnp.bfloat16)


def scores_of(left, right):
    return lax.dot_general(left, right, (((1,), (1,)), ((), ())), preferred_element_type=jnp.float32)


def negative_coef(left, right, scale, bias):
    return (jax.nn.sigmoid(scale * scores_of(left, right) + bias) * scale).astype(jnp.bfloat16)


def each_columns(width, body, step=256):
    for start in range(0, width, step):
        body(slice(start, start + step))


def dot(coef, rows):
    return jnp.dot(coef, rows, preferred_element_type=jnp.float32)


def stack(out_ref, first, second):
    rows = first.shape[0]
    out_ref[:rows, :] = first
    out_ref[rows:, :] = second


def half(ref, part):
    rows = ref.shape[0] // 2
    return ref[part * rows : (part + 1) * rows, :]


def near_x_kernel(
    scale_ref, bias_ref, own, x_far, y_far, mate, cross, acc, coef_t, x, y, near
):
    rows = own.shape[0] // 2
    scale, bias = scale_ref[0], bias_ref[0]
    stack(x, half(own, 0), x_far[...])
    stack(y, half(own, 1), y_far[...])
    stack(near, half(mate, 0), half(cross, 0))
    shape = (2 * rows, 2 * rows)
    first = lax.broadcasted_iota(jnp.int32, shape, 0)
    positive = (first == lax.broadcasted_iota(jnp.int32, shape, 1)) & (first < rows)
    logits = scale * scores_of(x[...], y[...]) + bias
    size = jax.nn.sigmoid(jnp.where(positive, -logits, logits)) * scale
    signed = jnp.where(positive, -size, size)
    coef_own = signed.astype(jnp.bfloat16)
    coef_t[...] = signed.T.astype(jnp.bfloat16)
    coef = negative_coef(x[...], near[...], scale, bias)

    def body(cols):
        acc[:, cols] = dot(coef_own, y[:, cols]) + dot(coef, near[:, cols])

    each_columns(own.shape[1], body)


def near_y_kernel(scale_ref, bias_ref, x, y, mate, cross, coef_t, after, acc, near):
    del after
    stack(near, half(mate, 1), half(cross, 1))
    coef = negative_coef(y[...], near[...], scale_ref[0], bias_ref[0])

    def body(cols):
        acc[:, cols] = dot(coef_t[...], x[:, cols]) + dot(coef, near[:, cols])

    each_columns(x.shape[1], body)


def far_kernel(scale_ref, bias_ref, side, cross, mate, acc, kept, sent, near):
    rows = kept.shape[0]
    stack(near, mate[...], cross[...])
    coef = negative_coef(side[...], near[...], scale_ref[0], bias_ref[0])

    def body(cols):
        total = acc[:, cols] + dot(coef, near[:, cols])
        kept[:, cols] = total[:rows]
        sent[:, cols] = total[rows:].astype(jnp.bfloat16)

    each_columns(side.shape[1], body)


def grad_strip(raw, direction):
    values = raw.astype(jnp.float32)
    inverse = inverse_of(values)
    norm = values * inverse
    inner = jnp.sum(norm * direction, axis=-1, keepdims=True)
    return ((direction - norm * inner) * inverse).astype(jnp.bfloat16)


def first_grad_kernel(odd_ref, img_raw, txt_raw, kept, there, out):
    odd = odd_ref[0] > 0
    for start in range(0, img_raw.shape[0], STRIP):
        here = slice(start, start + STRIP)
        raw = jnp.where(odd, txt_raw[here, :], img_raw[here, :])
        out[here, :] = grad_strip(raw, kept[here, :] + there[here, :].astype(jnp.float32))


def second_grad_kernel(odd_ref, img_raw, txt_raw, kept, there, x_grad, img_grad, txt_grad):
    odd = odd_ref[0] > 0
    for start in range(0, img_raw.shape[0], STRIP):
        here = slice(start, start + STRIP)
        raw = jnp.where(odd, img_raw[here, :], txt_raw[here, :])
        y = grad_strip(raw, kept[here, :] + there[here, :].astype(jnp.float32))
        x = x_grad[here, :]
        img_grad[here, :] = jnp.where(odd, y, x)
        txt_grad[here, :] = jnp.where(odd, x, y)


def call(kernel, outs, scalars, arrays, scratch=(), flops=0, there=()):
    moved = sum(a.size * a.dtype.itemsize for a in arrays)
    return pl.pallas_call(
        kernel,
        out_shape=outs,
        in_specs=[pl.BlockSpec(memory_space=pltpu.SMEM)] * len(scalars)
        + [pl.BlockSpec(memory_space=pltpu.VMEM)] * len(arrays)
        + [pl.BlockSpec(memory_space=pl.ANY)] * len(there),
        out_specs=jax.tree.map(lambda _: pl.BlockSpec(memory_space=pltpu.VMEM), outs),
        scratch_shapes=list(scratch),
        compiler_params=pltpu.CompilerParams(vmem_limit_bytes=VMEM_LIMIT),
        cost_estimate=pl.CostEstimate(flops=flops, bytes_accessed=moved, transcendentals=0),
    )(*scalars, *arrays, *there)


def local(img_raw, txt_raw, logit_scale, logit_bias, moves):
    first, second, to_mate, to_cross = moves
    rows, width = img_raw.shape
    odd = (lax.axis_index("dp") & 1).astype(jnp.int32).reshape(1)
    scalars = (logit_scale.reshape(1), logit_bias.reshape(1))
    low_shape = jax.ShapeDtypeStruct((2 * rows, width), jnp.bfloat16)
    acc_shape = jax.ShapeDtypeStruct((2 * rows, width), jnp.float32)
    own_shape = jax.ShapeDtypeStruct((rows, width), jnp.float32)
    sent_shape = jax.ShapeDtypeStruct((rows, width), jnp.bfloat16)
    coef_shape = jax.ShapeDtypeStruct((2 * rows, 2 * rows), jnp.bfloat16)
    pair = pltpu.VMEM((2 * rows, width), jnp.bfloat16)
    unit = 2 * (2 * rows) * (2 * rows) * width

    x = jnp.where(odd > 0, txt_raw, img_raw)
    y = jnp.where(odd > 0, img_raw, txt_raw)
    x_there = lax.ppermute(x, AXES, first)
    y_there = lax.ppermute(y, AXES, second)
    own = call(low_kernel, low_shape, (), (x, y))
    cross_own = lax.ppermute(own, AXES, to_cross)
    mate_own = lax.ppermute(own, AXES, to_mate)
    x_far = call(one_low_kernel, sent_shape, (), (x_there,))
    x_cross = lax.ppermute(x_far, AXES, to_cross)
    x_mate = lax.ppermute(x_far, AXES, to_mate)
    y_far = call(one_low_kernel, sent_shape, (), (y_there,))
    y_cross = lax.ppermute(y_far, AXES, to_cross)
    y_mate = lax.ppermute(y_far, AXES, to_mate)
    x_acc, coef_t, x_half, y_half = call(
        near_x_kernel,
        (acc_shape, coef_shape, low_shape, low_shape),
        scalars,
        (own, x_far, y_far, mate_own, cross_own),
        [pair],
        4 * unit,
    )
    x_kept, x_sent = call(
        far_kernel,
        (own_shape, sent_shape),
        scalars,
        (x_half, x_cross, x_mate, x_acc),
        [pair],
        2 * unit,
    )
    y_acc = call(
        near_y_kernel,
        acc_shape,
        scalars,
        (x_half, y_half, mate_own, cross_own, coef_t),
        [pair],
        3 * unit,
        (x_sent,),
    )
    y_kept, y_sent = call(
        far_kernel,
        (own_shape, sent_shape),
        scalars,
        (y_half, y_cross, y_mate, y_acc),
        [pair],
        2 * unit,
    )
    x_back = lax.ppermute(x_sent, AXES, first)
    y_back = lax.ppermute(y_sent, AXES, second)
    x_grad = call(first_grad_kernel, sent_shape, (odd,), (img_raw, txt_raw, x_kept, x_back))
    return call(
        second_grad_kernel,
        (sent_shape, sent_shape),
        (odd,),
        (img_raw, txt_raw, y_kept, y_back, x_grad),
    )


def solution(mesh):
    moves = routes(mesh.shape["dp"], mesh.shape["fsdp"])
    in_specs = (P(AXES, None), P(AXES, None), P(), P())
    out_specs = (P(AXES, None), P(AXES, None))

    def step(*args):
        return local(*args, moves)

    return jax.shard_map(step, mesh=mesh, in_specs=in_specs, out_specs=out_specs, check_vma=False)
```

```python
import functools

import jax
import jax.numpy as jnp
from jax import lax
from jax.experimental import pallas as pl
from jax.experimental.pallas import tpu as pltpu
from jax.sharding import PartitionSpec as P

AXES = ("dp", "fsdp")
SPAN = 16
STRIP = 32
VMEM_LIMIT = 10 * 1024 * 1024


def device_of(block, role, blocks, ways):
    block = block % blocks
    return block * ways + (role + block // SPAN) % ways


def routes(blocks, ways):
    first, second, mate, cross = [], [], [], []
    for block in range(blocks):
        for role in range(ways):
            here = device_of(block, role, blocks, ways)
            img = device_of(block, role ^ 1, blocks, ways)
            txt = device_of(block, ways - 1 - role, blocks, ways)
            across = block + 1 if block % 2 else block - 1
            first.append((here, txt if block % 2 else img))
            second.append((here, img if block % 2 else txt))
            mate.append((here, device_of(block ^ 1, role, blocks, ways)))
            cross.append((here, device_of(across, role, blocks, ways)))
    return first, second, mate, cross


def inverse_of(values):
    return lax.rsqrt(jnp.sum(values * values, axis=-1, keepdims=True) + 1e-06)


def low_kernel(x_ref, y_ref, low_ref):
    rows = x_ref.shape[0]
    for part, ref in enumerate((x_ref, y_ref)):
        for start in range(0, rows, STRIP):
            values = ref[start : start + STRIP, :].astype(jnp.float32)
            strip = (values * inverse_of(values)).astype(jnp.bfloat16)
            low_ref[part * rows + start : part * rows + start + STRIP, :] = strip


def scores_of(left, right):
    return lax.dot_general(left, right, (((1,), (1,)), ((), ())), preferred_element_type=jnp.float32)


def negative_coef(left, right, scale, bias):
    return (jax.nn.sigmoid(scale * scores_of(left, right) + bias) * scale).astype(jnp.bfloat16)


def each_columns(width, body, step=256):
    for start in range(0, width, step):
        body(slice(start, start + step))


def dot(coef, rows):
    return jnp.dot(coef, rows, preferred_element_type=jnp.float32)


def stack(out_ref, first, second):
    rows = first.shape[0]
    out_ref[:rows, :] = first
    out_ref[rows:, :] = second


def half(ref, part):
    rows = ref.shape[0] // 2
    return ref[part * rows : (part + 1) * rows, :]


def near_x_kernel(scale_ref, bias_ref, own, far, mate, cross, acc, coef_t, x, y, near):
    rows = own.shape[0] // 2
    scale, bias = scale_ref[0], bias_ref[0]
    stack(x, half(own, 0), half(far, 0))
    stack(y, half(own, 1), half(far, 1))
    stack(near, half(mate, 0), half(cross, 0))
    shape = (2 * rows, 2 * rows)
    first = lax.broadcasted_iota(jnp.int32, shape, 0)
    positive = (first == lax.broadcasted_iota(jnp.int32, shape, 1)) & (first < rows)
    logits = scale * scores_of(x[...], y[...]) + bias
    size = jax.nn.sigmoid(jnp.where(positive, -logits, logits)) * scale
    signed = jnp.where(positive, -size, size)
    coef_own = signed.astype(jnp.bfloat16)
    coef_t[...] = signed.T.astype(jnp.bfloat16)
    coef = negative_coef(x[...], near[...], scale, bias)

    def body(cols):
        acc[:, cols] = dot(coef_own, y[:, cols]) + dot(coef, near[:, cols])

    each_columns(own.shape[1], body)


def near_y_kernel(scale_ref, bias_ref, x, y, mate, cross, coef_t, after, acc, near):
    del after
    stack(near, half(mate, 1), half(cross, 1))
    coef = negative_coef(y[...], near[...], scale_ref[0], bias_ref[0])

    def body(cols):
        acc[:, cols] = dot(coef_t[...], x[:, cols]) + dot(coef, near[:, cols])

    each_columns(x.shape[1], body)


def far_kernel(part, scale_ref, bias_ref, side, cross, mate, acc, kept, sent, near):
    rows = kept.shape[0]
    stack(near, half(mate, part), cross[...])
    coef = negative_coef(side[...], near[...], scale_ref[0], bias_ref[0])

    def body(cols):
        total = acc[:, cols] + dot(coef, near[:, cols])
        kept[:, cols] = total[:rows]
        sent[:, cols] = total[rows:].astype(jnp.bfloat16)

    each_columns(side.shape[1], body)


def grad_strip(raw, direction):
    values = raw.astype(jnp.float32)
    inverse = inverse_of(values)
    norm = values * inverse
    inner = jnp.sum(norm * direction, axis=-1, keepdims=True)
    return ((direction - norm * inner) * inverse).astype(jnp.bfloat16)


def first_grad_kernel(odd_ref, img_raw, txt_raw, kept, there, out):
    odd = odd_ref[0] > 0
    for start in range(0, img_raw.shape[0], STRIP):
        here = slice(start, start + STRIP)
        raw = jnp.where(odd, txt_raw[here, :], img_raw[here, :])
        out[here, :] = grad_strip(raw, kept[here, :] + there[here, :].astype(jnp.float32))


def second_grad_kernel(odd_ref, img_raw, txt_raw, kept, there, x_grad, img_grad, txt_grad):
    odd = odd_ref[0] > 0
    for start in range(0, img_raw.shape[0], STRIP):
        here = slice(start, start + STRIP)
        raw = jnp.where(odd, img_raw[here, :], txt_raw[here, :])
        y = grad_strip(raw, kept[here, :] + there[here, :].astype(jnp.float32))
        x = x_grad[here, :]
        img_grad[here, :] = jnp.where(odd, y, x)
        txt_grad[here, :] = jnp.where(odd, x, y)


def call(kernel, outs, scalars, arrays, scratch=(), flops=0, there=()):
    moved = sum(a.size * a.dtype.itemsize for a in arrays)
    return pl.pallas_call(
        kernel,
        out_shape=outs,
        in_specs=[pl.BlockSpec(memory_space=pltpu.SMEM)] * len(scalars)
        + [pl.BlockSpec(memory_space=pltpu.VMEM)] * len(arrays)
        + [pl.BlockSpec(memory_space=pl.ANY)] * len(there),
        out_specs=jax.tree.map(lambda _: pl.BlockSpec(memory_space=pltpu.VMEM), outs),
        scratch_shapes=list(scratch),
        compiler_params=pltpu.CompilerParams(vmem_limit_bytes=VMEM_LIMIT),
        cost_estimate=pl.CostEstimate(flops=flops, bytes_accessed=moved, transcendentals=0),
    )(*scalars, *arrays, *there)


def local(img_raw, txt_raw, logit_scale, logit_bias, moves):
    first, second, to_mate, to_cross = moves
    rows, width = img_raw.shape
    odd = (lax.axis_index("dp") & 1).astype(jnp.int32).reshape(1)
    scalars = (logit_scale.reshape(1), logit_bias.reshape(1))
    low_shape = jax.ShapeDtypeStruct((2 * rows, width), jnp.bfloat16)
    acc_shape = jax.ShapeDtypeStruct((2 * rows, width), jnp.float32)
    own_shape = jax.ShapeDtypeStruct((rows, width), jnp.float32)
    sent_shape = jax.ShapeDtypeStruct((rows, width), jnp.bfloat16)
    coef_shape = jax.ShapeDtypeStruct((2 * rows, 2 * rows), jnp.bfloat16)
    pair = pltpu.VMEM((2 * rows, width), jnp.bfloat16)
    unit = 2 * (2 * rows) * (2 * rows) * width

    x = jnp.where(odd > 0, txt_raw, img_raw)
    y = jnp.where(odd > 0, img_raw, txt_raw)
    x_there = lax.ppermute(x, AXES, first)
    y_there = lax.ppermute(y, AXES, second)
    own = call(low_kernel, low_shape, (), (x, y))
    cross_own = lax.ppermute(own, AXES, to_cross)
    mate_own = lax.ppermute(own, AXES, to_mate)
    far = call(low_kernel, low_shape, (), (x_there, y_there))
    x_far, y_far = far[:rows], far[rows:]
    x_cross = lax.ppermute(x_far, AXES, to_cross)
    mate_far = lax.ppermute(far, AXES, to_mate)
    y_cross = lax.ppermute(y_far, AXES, to_cross)
    x_acc, coef_t, x_half, y_half = call(
        near_x_kernel,
        (acc_shape, coef_shape, low_shape, low_shape),
        scalars,
        (own, far, mate_own, cross_own),
        [pair],
        4 * unit,
    )
    x_kept, x_sent = call(
        functools.partial(far_kernel, 0),
        (own_shape, sent_shape),
        scalars,
        (x_half, x_cross, mate_far, x_acc),
        [pair],
        2 * unit,
    )
    y_acc = call(
        near_y_kernel,
        acc_shape,
        scalars,
        (x_half, y_half, mate_own, cross_own, coef_t),
        [pair],
        3 * unit,
        (x_sent,),
    )
    y_kept, y_sent = call(
        functools.partial(far_kernel, 1),
        (own_shape, sent_shape),
        scalars,
        (y_half, y_cross, mate_far, y_acc),
        [pair],
        2 * unit,
    )
    x_back = lax.ppermute(x_sent, AXES, first)
    y_back = lax.ppermute(y_sent, AXES, second)
    x_grad = call(first_grad_kernel, sent_shape, (odd,), (img_raw, txt_raw, x_kept, x_back))
    return call(
        second_grad_kernel,
        (sent_shape, sent_shape),
        (odd,),
        (img_raw, txt_raw, y_kept, y_back, x_grad),
    )


def solution(mesh):
    moves = routes(mesh.shape["dp"], mesh.shape["fsdp"])
    in_specs = (P(AXES, None), P(AXES, None), P(), P())
    out_specs = (P(AXES, None), P(AXES, None))

    def step(*args):
        return local(*args, moves)

    return jax.shard_map(step, mesh=mesh, in_specs=in_specs, out_specs=out_specs, check_vma=False)
```

```python
import functools

import jax
import jax.numpy as jnp
from jax import lax
from jax.experimental import pallas as pl
from jax.experimental.pallas import tpu as pltpu
from jax.sharding import PartitionSpec as P

AXES = ("dp", "fsdp")
SPAN = 16
STRIP = 32
VMEM_LIMIT = 10 * 1024 * 1024


def device_of(block, role, blocks, ways):
    block = block % blocks
    return block * ways + (role + block // SPAN) % ways


def routes(blocks, ways):
    first, second, mate, cross = [], [], [], []
    for block in range(blocks):
        for role in range(ways):
            here = device_of(block, role, blocks, ways)
            img = device_of(block, role ^ 1, blocks, ways)
            txt = device_of(block, ways - 1 - role, blocks, ways)
            across = block + 1 if block % 2 else block - 1
            first.append((here, txt if block % 2 else img))
            second.append((here, img if block % 2 else txt))
            mate.append((here, device_of(block ^ 1, role, blocks, ways)))
            cross.append((here, device_of(across, role, blocks, ways)))
    return first, second, mate, cross


def inverse_of(values):
    return lax.rsqrt(jnp.sum(values * values, axis=-1, keepdims=True) + 1e-06)


def low_kernel(x_ref, y_ref, low_ref):
    rows = x_ref.shape[0]
    for part, ref in enumerate((x_ref, y_ref)):
        for start in range(0, rows, STRIP):
            values = ref[start : start + STRIP, :].astype(jnp.float32)
            strip = (values * inverse_of(values)).astype(jnp.bfloat16)
            low_ref[part * rows + start : part * rows + start + STRIP, :] = strip


def scores_of(left, right):
    return lax.dot_general(left, right, (((1,), (1,)), ((), ())), preferred_element_type=jnp.float32)


def negative_coef(left, right, scale, bias):
    return (jax.nn.sigmoid(scale * scores_of(left, right) + bias) * scale).astype(jnp.bfloat16)


def each_columns(width, body, step=256):
    for start in range(0, width, step):
        body(slice(start, start + step))


def dot(coef, rows):
    return jnp.dot(coef, rows, preferred_element_type=jnp.float32)


def stack(out_ref, first, second):
    rows = first.shape[0]
    out_ref[:rows, :] = first
    out_ref[rows:, :] = second


def half(ref, part):
    rows = ref.shape[0] // 2
    return ref[part * rows : (part + 1) * rows, :]


def near_x_kernel(scale_ref, bias_ref, own, far, mate, cross, acc, coef_t, x, y, near):
    rows = own.shape[0] // 2
    scale, bias = scale_ref[0], bias_ref[0]
    stack(x, half(own, 0), half(far, 0))
    stack(y, half(own, 1), half(far, 1))
    stack(near, half(mate, 0), half(cross, 0))
    shape = (2 * rows, 2 * rows)
    first = lax.broadcasted_iota(jnp.int32, shape, 0)
    positive = (first == lax.broadcasted_iota(jnp.int32, shape, 1)) & (first < rows)
    logits = scale * scores_of(x[...], y[...]) + bias
    size = jax.nn.sigmoid(jnp.where(positive, -logits, logits)) * scale
    signed = jnp.where(positive, -size, size)
    coef_own = signed.astype(jnp.bfloat16)
    coef_t[...] = signed.T.astype(jnp.bfloat16)
    coef = negative_coef(x[...], near[...], scale, bias)

    def body(cols):
        acc[:, cols] = dot(coef_own, y[:, cols]) + dot(coef, near[:, cols])

    each_columns(own.shape[1], body)


def near_y_kernel(scale_ref, bias_ref, x, y, mate, cross, coef_t, after, acc, near):
    del after
    stack(near, half(mate, 1), half(cross, 1))
    coef = negative_coef(y[...], near[...], scale_ref[0], bias_ref[0])

    def body(cols):
        acc[:, cols] = dot(coef_t[...], x[:, cols]) + dot(coef, near[:, cols])

    each_columns(x.shape[1], body)


def far_kernel(part, scale_ref, bias_ref, side, acc, cross, mate, kept, sent, near, sems):
    rows = kept.shape[0]
    copies = [
        pltpu.make_async_copy(mate.at[pl.ds(part * rows, rows), :], near.at[pl.ds(0, rows), :], sems.at[0]),
        pltpu.make_async_copy(cross, near.at[pl.ds(rows, rows), :], sems.at[1]),
    ]
    for copy in copies:
        copy.start()
    for copy in copies:
        copy.wait()
    coef = negative_coef(side[...], near[...], scale_ref[0], bias_ref[0])

    def body(cols):
        total = acc[:, cols] + dot(coef, near[:, cols])
        kept[:, cols] = total[:rows]
        sent[:, cols] = total[rows:].astype(jnp.bfloat16)

    each_columns(side.shape[1], body)


def grad_strip(raw, direction):
    values = raw.astype(jnp.float32)
    inverse = inverse_of(values)
    norm = values * inverse
    inner = jnp.sum(norm * direction, axis=-1, keepdims=True)
    return ((direction - norm * inner) * inverse).astype(jnp.bfloat16)


def first_grad_kernel(odd_ref, img_raw, txt_raw, kept, there, out):
    odd = odd_ref[0] > 0
    for start in range(0, img_raw.shape[0], STRIP):
        here = slice(start, start + STRIP)
        raw = jnp.where(odd, txt_raw[here, :], img_raw[here, :])
        out[here, :] = grad_strip(raw, kept[here, :] + there[here, :].astype(jnp.float32))


def second_grad_kernel(odd_ref, img_raw, txt_raw, kept, there, x_grad, img_grad, txt_grad):
    odd = odd_ref[0] > 0
    for start in range(0, img_raw.shape[0], STRIP):
        here = slice(start, start + STRIP)
        raw = jnp.where(odd, img_raw[here, :], txt_raw[here, :])
        y = grad_strip(raw, kept[here, :] + there[here, :].astype(jnp.float32))
        x = x_grad[here, :]
        img_grad[here, :] = jnp.where(odd, y, x)
        txt_grad[here, :] = jnp.where(odd, x, y)


def call(kernel, outs, scalars, arrays, scratch=(), flops=0, there=()):
    moved = sum(a.size * a.dtype.itemsize for a in arrays)
    return pl.pallas_call(
        kernel,
        out_shape=outs,
        in_specs=[pl.BlockSpec(memory_space=pltpu.SMEM)] * len(scalars)
        + [pl.BlockSpec(memory_space=pltpu.VMEM)] * len(arrays)
        + [pl.BlockSpec(memory_space=pl.ANY)] * len(there),
        out_specs=jax.tree.map(lambda _: pl.BlockSpec(memory_space=pltpu.VMEM), outs),
        scratch_shapes=list(scratch),
        compiler_params=pltpu.CompilerParams(vmem_limit_bytes=VMEM_LIMIT),
        cost_estimate=pl.CostEstimate(flops=flops, bytes_accessed=moved, transcendentals=0),
    )(*scalars, *arrays, *there)


def local(img_raw, txt_raw, logit_scale, logit_bias, moves):
    first, second, to_mate, to_cross = moves
    rows, width = img_raw.shape
    odd = (lax.axis_index("dp") & 1).astype(jnp.int32).reshape(1)
    scalars = (logit_scale.reshape(1), logit_bias.reshape(1))
    low_shape = jax.ShapeDtypeStruct((2 * rows, width), jnp.bfloat16)
    acc_shape = jax.ShapeDtypeStruct((2 * rows, width), jnp.float32)
    own_shape = jax.ShapeDtypeStruct((rows, width), jnp.float32)
    sent_shape = jax.ShapeDtypeStruct((rows, width), jnp.bfloat16)
    coef_shape = jax.ShapeDtypeStruct((2 * rows, 2 * rows), jnp.bfloat16)
    pair, sems = pltpu.VMEM((2 * rows, width), jnp.bfloat16), pltpu.SemaphoreType.DMA((2,))
    unit = 2 * (2 * rows) * (2 * rows) * width

    x = jnp.where(odd > 0, txt_raw, img_raw)
    y = jnp.where(odd > 0, img_raw, txt_raw)
    x_there = lax.ppermute(x, AXES, first)
    y_there = lax.ppermute(y, AXES, second)
    own = call(low_kernel, low_shape, (), (x, y))
    cross_own = lax.ppermute(own, AXES, to_cross)
    mate_own = lax.ppermute(own, AXES, to_mate)
    far = call(low_kernel, low_shape, (), (x_there, y_there))
    x_far, y_far = far[:rows], far[rows:]
    x_cross = lax.ppermute(x_far, AXES, to_cross)
    mate_far = lax.ppermute(far, AXES, to_mate)
    y_cross = lax.ppermute(y_far, AXES, to_cross)
    x_acc, coef_t, x_half, y_half = call(
        near_x_kernel,
        (acc_shape, coef_shape, low_shape, low_shape),
        scalars,
        (own, far, mate_own, cross_own),
        [pair],
        4 * unit,
    )
    x_kept, x_sent = call(
        functools.partial(far_kernel, 0),
        (own_shape, sent_shape),
        scalars,
        (x_half, x_acc),
        [pair, sems],
        2 * unit,
        (x_cross, mate_far),
    )
    y_acc = call(
        near_y_kernel,
        acc_shape,
        scalars,
        (x_half, y_half, mate_own, cross_own, coef_t),
        [pair],
        3 * unit,
        (x_sent,),
    )
    y_kept, y_sent = call(
        functools.partial(far_kernel, 1),
        (own_shape, sent_shape),
        scalars,
        (y_half, y_acc),
        [pair, sems],
        2 * unit,
        (y_cross, mate_far),
    )
    x_back = lax.ppermute(x_sent, AXES, first)
    y_back = lax.ppermute(y_sent, AXES, second)
    x_grad = call(first_grad_kernel, sent_shape, (odd,), (img_raw, txt_raw, x_kept, x_back))
    return call(
        second_grad_kernel,
        (sent_shape, sent_shape),
        (odd,),
        (img_raw, txt_raw, y_kept, y_back, x_grad),
    )


def solution(mesh):
    moves = routes(mesh.shape["dp"], mesh.shape["fsdp"])
    in_specs = (P(AXES, None), P(AXES, None), P(), P())
    out_specs = (P(AXES, None), P(AXES, None))

    def step(*args):
        return local(*args, moves)

    return jax.shard_map(step, mesh=mesh, in_specs=in_specs, out_specs=out_specs, check_vma=False)
```

```python
import functools

import jax
import jax.numpy as jnp
from jax import lax
from jax.experimental import pallas as pl
from jax.experimental.pallas import tpu as pltpu
from jax.sharding import PartitionSpec as P

AXES = ("dp", "fsdp")
SPAN = 16
STRIP = 32
VMEM_LIMIT = 10 * 1024 * 1024


def device_of(block, role, blocks, ways):
    block = block % blocks
    return block * ways + (role + block // SPAN) % ways


def routes(blocks, ways):
    first, second, mate, cross = [], [], [], []
    for block in range(blocks):
        for role in range(ways):
            here = device_of(block, role, blocks, ways)
            img = device_of(block, role ^ 1, blocks, ways)
            txt = device_of(block, ways - 1 - role, blocks, ways)
            across = block + 1 if block % 2 else block - 1
            first.append((here, txt if block % 2 else img))
            second.append((here, img if block % 2 else txt))
            mate.append((here, device_of(block ^ 1, role, blocks, ways)))
            cross.append((here, device_of(across, role, blocks, ways)))
    return first, second, mate, cross


def inverse_of(values):
    return lax.rsqrt(jnp.sum(values * values, axis=-1, keepdims=True) + 1e-06)


def low_kernel(x_ref, y_ref, low_ref):
    rows = x_ref.shape[0]
    for part, ref in enumerate((x_ref, y_ref)):
        for start in range(0, rows, STRIP):
            values = ref[start : start + STRIP, :].astype(jnp.float32)
            strip = (values * inverse_of(values)).astype(jnp.bfloat16)
            low_ref[part * rows + start : part * rows + start + STRIP, :] = strip


def scores_of(left, right):
    return lax.dot_general(left, right, (((1,), (1,)), ((), ())), preferred_element_type=jnp.float32)


def negative_coef(left, right, scale, bias):
    return (jax.nn.sigmoid(scale * scores_of(left, right) + bias) * scale).astype(jnp.bfloat16)


def each_columns(width, body, step=256):
    for start in range(0, width, step):
        body(slice(start, start + step))


def dot(coef, rows):
    return jnp.dot(coef, rows, preferred_element_type=jnp.float32)


def stack(out_ref, first, second):
    rows = first.shape[0]
    out_ref[:rows, :] = first
    out_ref[rows:, :] = second


def half(ref, part):
    rows = ref.shape[0] // 2
    return ref[part * rows : (part + 1) * rows, :]


def near_x_kernel(scale_ref, bias_ref, own, far, mate, cross, acc, coef_t, x, y, near):
    rows = own.shape[0] // 2
    scale, bias = scale_ref[0], bias_ref[0]
    stack(x, half(own, 0), half(far, 0))
    stack(y, half(own, 1), half(far, 1))
    stack(near, half(mate, 0), half(cross, 0))
    shape = (2 * rows, 2 * rows)
    first = lax.broadcasted_iota(jnp.int32, shape, 0)
    positive = (first == lax.broadcasted_iota(jnp.int32, shape, 1)) & (first < rows)
    logits = scale * scores_of(x[...], y[...]) + bias
    size = jax.nn.sigmoid(jnp.where(positive, -logits, logits)) * scale
    signed = jnp.where(positive, -size, size)
    coef_own = signed.astype(jnp.bfloat16)
    coef_t[...] = signed.T.astype(jnp.bfloat16)
    coef = negative_coef(x[...], near[...], scale, bias)

    def body(cols):
        acc[:, cols] = dot(coef_own, y[:, cols]) + dot(coef, near[:, cols])

    each_columns(own.shape[1], body)


def near_y_kernel(scale_ref, bias_ref, x, y, mate, cross, coef_t, after, acc, near):
    del after
    stack(near, half(mate, 1), half(cross, 1))
    coef = negative_coef(y[...], near[...], scale_ref[0], bias_ref[0])

    def body(cols):
        acc[:, cols] = dot(coef_t[...], x[:, cols]) + dot(coef, near[:, cols])

    each_columns(x.shape[1], body)


def far_kernel(part, scale_ref, bias_ref, side, cross, mate, acc, kept, sent, near):
    rows = kept.shape[0]
    stack(near, half(mate, part), cross[...])
    coef = negative_coef(side[...], near[...], scale_ref[0], bias_ref[0])

    def body(cols):
        total = acc[:, cols] + dot(coef, near[:, cols])
        kept[:, cols] = total[:rows]
        sent[:, cols] = total[rows:].astype(jnp.bfloat16)

    each_columns(side.shape[1], body)


def grad_strip(raw, direction):
    values = raw.astype(jnp.float32)
    inverse = inverse_of(values)
    norm = values * inverse
    inner = jnp.sum(norm * direction, axis=-1, keepdims=True)
    return ((direction - norm * inner) * inverse).astype(jnp.bfloat16)


def first_grad_kernel(odd_ref, img_raw, txt_raw, kept, there, out):
    odd = odd_ref[0] > 0
    for start in range(0, img_raw.shape[0], STRIP):
        here = slice(start, start + STRIP)
        raw = jnp.where(odd, txt_raw[here, :], img_raw[here, :])
        out[here, :] = grad_strip(raw, kept[here, :] + there[here, :].astype(jnp.float32))


def second_grad_kernel(
    odd_ref, img_raw, txt_raw, kept, there, x_grad, img_grad, txt_grad, y_grad, sems
):
    def run(raw, x_out, y_out):
        copies = [pltpu.make_async_copy(x_grad, x_out, sems.at[0])]
        copies[0].start()
        for place in range(raw.shape[0] // STRIP):
            here = slice(place * STRIP, (place + 1) * STRIP)
            y = grad_strip(raw[here, :], kept[here, :] + there[here, :].astype(jnp.float32))
            y_grad[here, :] = y
            strip = pl.ds(place * STRIP, STRIP)
            source, out = y_grad.at[strip, :], y_out.at[strip, :]
            copies.append(pltpu.make_async_copy(source, out, sems.at[place + 1]))
            copies[-1].start()
        for copy in copies:
            copy.wait()

    @pl.when(odd_ref[0] == 0)
    def _():
        run(txt_raw, img_grad, txt_grad)

    @pl.when(odd_ref[0] != 0)
    def _():
        run(img_raw, txt_grad, img_grad)


def last(odd, *arrays):
    shape = arrays[0].shape
    out = jax.ShapeDtypeStruct(shape, jnp.bfloat16)
    return pl.pallas_call(
        second_grad_kernel,
        out_shape=(out, out),
        in_specs=[pl.BlockSpec(memory_space=pltpu.SMEM)]
        + [pl.BlockSpec(memory_space=pltpu.VMEM)] * len(arrays),
        out_specs=(pl.BlockSpec(memory_space=pl.ANY),) * 2,
        scratch_shapes=[
            pltpu.VMEM(shape, jnp.bfloat16),
            pltpu.SemaphoreType.DMA((1 + shape[0] // STRIP,)),
        ],
        compiler_params=pltpu.CompilerParams(vmem_limit_bytes=VMEM_LIMIT),
    )(odd, *arrays)


def call(kernel, outs, scalars, arrays, scratch=(), flops=0, there=()):
    moved = sum(a.size * a.dtype.itemsize for a in arrays)
    return pl.pallas_call(
        kernel,
        out_shape=outs,
        in_specs=[pl.BlockSpec(memory_space=pltpu.SMEM)] * len(scalars)
        + [pl.BlockSpec(memory_space=pltpu.VMEM)] * len(arrays)
        + [pl.BlockSpec(memory_space=pl.ANY)] * len(there),
        out_specs=jax.tree.map(lambda _: pl.BlockSpec(memory_space=pltpu.VMEM), outs),
        scratch_shapes=list(scratch),
        compiler_params=pltpu.CompilerParams(vmem_limit_bytes=VMEM_LIMIT),
        cost_estimate=pl.CostEstimate(flops=flops, bytes_accessed=moved, transcendentals=0),
    )(*scalars, *arrays, *there)


def local(img_raw, txt_raw, logit_scale, logit_bias, moves):
    first, second, to_mate, to_cross = moves
    rows, width = img_raw.shape
    odd = (lax.axis_index("dp") & 1).astype(jnp.int32).reshape(1)
    scalars = (logit_scale.reshape(1), logit_bias.reshape(1))
    low_shape = jax.ShapeDtypeStruct((2 * rows, width), jnp.bfloat16)
    acc_shape = jax.ShapeDtypeStruct((2 * rows, width), jnp.float32)
    own_shape = jax.ShapeDtypeStruct((rows, width), jnp.float32)
    sent_shape = jax.ShapeDtypeStruct((rows, width), jnp.bfloat16)
    coef_shape = jax.ShapeDtypeStruct((2 * rows, 2 * rows), jnp.bfloat16)
    pair = pltpu.VMEM((2 * rows, width), jnp.bfloat16)
    unit = 2 * (2 * rows) * (2 * rows) * width

    x = jnp.where(odd > 0, txt_raw, img_raw)
    y = jnp.where(odd > 0, img_raw, txt_raw)
    x_there = lax.ppermute(x, AXES, first)
    y_there = lax.ppermute(y, AXES, second)
    own = call(low_kernel, low_shape, (), (x, y))
    cross_own = lax.ppermute(own, AXES, to_cross)
    mate_own = lax.ppermute(own, AXES, to_mate)
    far = call(low_kernel, low_shape, (), (x_there, y_there))
    x_far, y_far = far[:rows], far[rows:]
    x_cross = lax.ppermute(x_far, AXES, to_cross)
    mate_far = lax.ppermute(far, AXES, to_mate)
    y_cross = lax.ppermute(y_far, AXES, to_cross)
    x_acc, coef_t, x_half, y_half = call(
        near_x_kernel,
        (acc_shape, coef_shape, low_shape, low_shape),
        scalars,
        (own, far, mate_own, cross_own),
        [pair],
        4 * unit,
    )
    x_kept, x_sent = call(
        functools.partial(far_kernel, 0),
        (own_shape, sent_shape),
        scalars,
        (x_half, x_cross, mate_far, x_acc),
        [pair],
        2 * unit,
    )
    y_acc = call(
        near_y_kernel,
        acc_shape,
        scalars,
        (x_half, y_half, mate_own, cross_own, coef_t),
        [pair],
        3 * unit,
        (x_sent,),
    )
    y_kept, y_sent = call(
        functools.partial(far_kernel, 1),
        (own_shape, sent_shape),
        scalars,
        (y_half, y_cross, mate_far, y_acc),
        [pair],
        2 * unit,
    )
    x_back = lax.ppermute(x_sent, AXES, first)
    y_back = lax.ppermute(y_sent, AXES, second)
    x_grad = call(first_grad_kernel, sent_shape, (odd,), (img_raw, txt_raw, x_kept, x_back))
    return last(odd, img_raw, txt_raw, y_kept, y_back, x_grad)


def solution(mesh):
    moves = routes(mesh.shape["dp"], mesh.shape["fsdp"])
    in_specs = (P(AXES, None), P(AXES, None), P(), P())
    out_specs = (P(AXES, None), P(AXES, None))

    def step(*args):
        return local(*args, moves)

    return jax.shard_map(step, mesh=mesh, in_specs=in_specs, out_specs=out_specs, check_vma=False)
```

```python
import functools

import jax
import jax.numpy as jnp
from jax import lax
from jax.experimental import pallas as pl
from jax.experimental.pallas import tpu as pltpu
from jax.sharding import PartitionSpec as P

AXES = ("dp", "fsdp")
SPAN = 16
STRIP = 32
VMEM_LIMIT = 10 * 1024 * 1024


def device_of(block, role, blocks, ways):
    block = block % blocks
    return block * ways + (role + block // SPAN) % ways


def routes(blocks, ways):
    first, second, mate, cross = [], [], [], []
    for block in range(blocks):
        for role in range(ways):
            here = device_of(block, role, blocks, ways)
            img = device_of(block, role ^ 1, blocks, ways)
            txt = device_of(block, ways - 1 - role, blocks, ways)
            across = block + 1 if block % 2 else block - 1
            first.append((here, txt if block % 2 else img))
            second.append((here, img if block % 2 else txt))
            mate.append((here, device_of(block ^ 1, role, blocks, ways)))
            cross.append((here, device_of(across, role, blocks, ways)))
    return first, second, mate, cross


def inverse_of(values):
    return lax.rsqrt(jnp.sum(values * values, axis=-1, keepdims=True) + 1e-06)


def low_kernel(x_ref, y_ref, low_ref):
    rows = x_ref.shape[0]
    for part, ref in enumerate((x_ref, y_ref)):
        for start in range(0, rows, STRIP):
            values = ref[start : start + STRIP, :].astype(jnp.float32)
            strip = (values * inverse_of(values)).astype(jnp.bfloat16)
            low_ref[part * rows + start : part * rows + start + STRIP, :] = strip


def scores_of(left, right):
    return lax.dot_general(left, right, (((1,), (1,)), ((), ())), preferred_element_type=jnp.float32)


def negative_coef(left, right, scale, bias):
    return (jax.nn.sigmoid(scale * scores_of(left, right) + bias) * scale).astype(jnp.bfloat16)


def each_columns(width, body, step=256):
    for start in range(0, width, step):
        body(slice(start, start + step))


def dot(coef, rows):
    return jnp.dot(coef, rows, preferred_element_type=jnp.float32)


def stack(out_ref, first, second):
    rows = first.shape[0]
    out_ref[:rows, :] = first
    out_ref[rows:, :] = second


def half(ref, part):
    rows = ref.shape[0] // 2
    return ref[part * rows : (part + 1) * rows, :]


def near_x_kernel(scale_ref, bias_ref, own, far, mate, cross, acc, coef_t, x, y, near):
    rows = own.shape[0] // 2
    scale, bias = scale_ref[0], bias_ref[0]
    stack(x, half(own, 0), half(far, 0))
    stack(y, half(own, 1), half(far, 1))
    stack(near, half(mate, 0), half(cross, 0))
    shape = (2 * rows, 2 * rows)
    first = lax.broadcasted_iota(jnp.int32, shape, 0)
    positive = (first == lax.broadcasted_iota(jnp.int32, shape, 1)) & (first < rows)
    logits = scale * scores_of(x[...], y[...]) + bias
    size = jax.nn.sigmoid(jnp.where(positive, -logits, logits)) * scale
    signed = jnp.where(positive, -size, size)
    coef_own = signed.astype(jnp.bfloat16)
    coef_t[...] = signed.T.astype(jnp.bfloat16)
    coef = negative_coef(x[...], near[...], scale, bias)

    def body(cols):
        acc[:, cols] = dot(coef_own, y[:, cols]) + dot(coef, near[:, cols])

    each_columns(own.shape[1], body)


def near_y_kernel(scale_ref, bias_ref, x, y, mate, cross, coef_t, after, acc, near):
    del after
    stack(near, half(mate, 1), half(cross, 1))
    coef = negative_coef(y[...], near[...], scale_ref[0], bias_ref[0])

    def body(cols):
        acc[:, cols] = dot(coef_t[...], x[:, cols]) + dot(coef, near[:, cols])

    each_columns(x.shape[1], body)


def far_kernel(part, scale_ref, bias_ref, side, acc, cross, mate, kept, sent, near, sems):
    rows = kept.shape[0]
    copies = [
        pltpu.make_async_copy(mate.at[pl.ds(part * rows, rows), :], near.at[pl.ds(0, rows), :], sems.at[0]),
        pltpu.make_async_copy(cross, near.at[pl.ds(rows, rows), :], sems.at[1]),
    ]
    for copy in copies:
        copy.start()
    for copy in copies:
        copy.wait()
    coef = negative_coef(side[...], near[...], scale_ref[0], bias_ref[0])

    def body(cols):
        total = acc[:, cols] + dot(coef, near[:, cols])
        kept[:, cols] = total[:rows]
        sent[:, cols] = total[rows:].astype(jnp.bfloat16)

    each_columns(side.shape[1], body)


def grad_strip(raw, direction):
    values = raw.astype(jnp.float32)
    inverse = inverse_of(values)
    norm = values * inverse
    inner = jnp.sum(norm * direction, axis=-1, keepdims=True)
    return ((direction - norm * inner) * inverse).astype(jnp.bfloat16)


def first_grad_kernel(odd_ref, img_raw, txt_raw, kept, there, out):
    odd = odd_ref[0] > 0
    for start in range(0, img_raw.shape[0], STRIP):
        here = slice(start, start + STRIP)
        raw = jnp.where(odd, txt_raw[here, :], img_raw[here, :])
        out[here, :] = grad_strip(raw, kept[here, :] + there[here, :].astype(jnp.float32))


def second_grad_kernel(
    odd_ref, img_raw, txt_raw, kept, there, x_grad, img_grad, txt_grad, y_grad, sems
):
    def run(raw, x_out, y_out):
        copies = [pltpu.make_async_copy(x_grad, x_out, sems.at[0])]
        copies[0].start()
        for place in range(raw.shape[0] // STRIP):
            here = slice(place * STRIP, (place + 1) * STRIP)
            y = grad_strip(raw[here, :], kept[here, :] + there[here, :].astype(jnp.float32))
            y_grad[here, :] = y
            strip = pl.ds(place * STRIP, STRIP)
            source, out = y_grad.at[strip, :], y_out.at[strip, :]
            copies.append(pltpu.make_async_copy(source, out, sems.at[place + 1]))
            copies[-1].start()
        for copy in copies:
            copy.wait()

    @pl.when(odd_ref[0] == 0)
    def _():
        run(txt_raw, img_grad, txt_grad)

    @pl.when(odd_ref[0] != 0)
    def _():
        run(img_raw, txt_grad, img_grad)


def last(odd, *arrays):
    shape = arrays[0].shape
    out = jax.ShapeDtypeStruct(shape, jnp.bfloat16)
    return pl.pallas_call(
        second_grad_kernel,
        out_shape=(out, out),
        in_specs=[pl.BlockSpec(memory_space=pltpu.SMEM)]
        + [pl.BlockSpec(memory_space=pltpu.VMEM)] * len(arrays),
        out_specs=(pl.BlockSpec(memory_space=pl.ANY),) * 2,
        scratch_shapes=[
            pltpu.VMEM(shape, jnp.bfloat16),
            pltpu.SemaphoreType.DMA((1 + shape[0] // STRIP,)),
        ],
        compiler_params=pltpu.CompilerParams(vmem_limit_bytes=VMEM_LIMIT),
    )(odd, *arrays)


def call(kernel, outs, scalars, arrays, scratch=(), flops=0, there=()):
    moved = sum(a.size * a.dtype.itemsize for a in arrays)
    return pl.pallas_call(
        kernel,
        out_shape=outs,
        in_specs=[pl.BlockSpec(memory_space=pltpu.SMEM)] * len(scalars)
        + [pl.BlockSpec(memory_space=pltpu.VMEM)] * len(arrays)
        + [pl.BlockSpec(memory_space=pl.ANY)] * len(there),
        out_specs=jax.tree.map(lambda _: pl.BlockSpec(memory_space=pltpu.VMEM), outs),
        scratch_shapes=list(scratch),
        compiler_params=pltpu.CompilerParams(vmem_limit_bytes=VMEM_LIMIT),
        cost_estimate=pl.CostEstimate(flops=flops, bytes_accessed=moved, transcendentals=0),
    )(*scalars, *arrays, *there)


def local(img_raw, txt_raw, logit_scale, logit_bias, moves):
    first, second, to_mate, to_cross = moves
    rows, width = img_raw.shape
    odd = (lax.axis_index("dp") & 1).astype(jnp.int32).reshape(1)
    scalars = (logit_scale.reshape(1), logit_bias.reshape(1))
    low_shape = jax.ShapeDtypeStruct((2 * rows, width), jnp.bfloat16)
    acc_shape = jax.ShapeDtypeStruct((2 * rows, width), jnp.float32)
    own_shape = jax.ShapeDtypeStruct((rows, width), jnp.float32)
    sent_shape = jax.ShapeDtypeStruct((rows, width), jnp.bfloat16)
    coef_shape = jax.ShapeDtypeStruct((2 * rows, 2 * rows), jnp.bfloat16)
    pair, sems = pltpu.VMEM((2 * rows, width), jnp.bfloat16), pltpu.SemaphoreType.DMA((2,))
    unit = 2 * (2 * rows) * (2 * rows) * width

    x = jnp.where(odd > 0, txt_raw, img_raw)
    y = jnp.where(odd > 0, img_raw, txt_raw)
    x_there = lax.ppermute(x, AXES, first)
    y_there = lax.ppermute(y, AXES, second)
    own = call(low_kernel, low_shape, (), (x, y))
    cross_own = lax.ppermute(own, AXES, to_cross)
    mate_own = lax.ppermute(own, AXES, to_mate)
    far = call(low_kernel, low_shape, (), (x_there, y_there))
    x_far, y_far = far[:rows], far[rows:]
    x_cross = lax.ppermute(x_far, AXES, to_cross)
    mate_far = lax.ppermute(far, AXES, to_mate)
    y_cross = lax.ppermute(y_far, AXES, to_cross)
    x_acc, coef_t, x_half, y_half = call(
        near_x_kernel,
        (acc_shape, coef_shape, low_shape, low_shape),
        scalars,
        (own, far, mate_own, cross_own),
        [pair],
        4 * unit,
    )
    x_kept, x_sent = call(
        functools.partial(far_kernel, 0),
        (own_shape, sent_shape),
        scalars,
        (x_half, x_acc),
        [pair, sems],
        2 * unit,
        (x_cross, mate_far),
    )
    y_acc = call(
        near_y_kernel,
        acc_shape,
        scalars,
        (x_half, y_half, mate_own, cross_own, coef_t),
        [pair],
        3 * unit,
        (x_sent,),
    )
    y_kept, y_sent = call(
        functools.partial(far_kernel, 1),
        (own_shape, sent_shape),
        scalars,
        (y_half, y_acc),
        [pair, sems],
        2 * unit,
        (y_cross, mate_far),
    )
    x_back = lax.ppermute(x_sent, AXES, first)
    y_back = lax.ppermute(y_sent, AXES, second)
    x_grad = call(first_grad_kernel, sent_shape, (odd,), (img_raw, txt_raw, x_kept, x_back))
    return last(odd, img_raw, txt_raw, y_kept, y_back, x_grad)


def solution(mesh):
    moves = routes(mesh.shape["dp"], mesh.shape["fsdp"])
    in_specs = (P(AXES, None), P(AXES, None), P(), P())
    out_specs = (P(AXES, None), P(AXES, None))

    def step(*args):
        return local(*args, moves)

    return jax.shard_map(step, mesh=mesh, in_specs=in_specs, out_specs=out_specs, check_vma=False)
```
